128 devices in a mesh: tmpl: 8 (over x_hi, z), spec: 8 (over y, x_lo), expo: 2 (over core).
Axes of the slice: x: 4 (x_hi: 2, x_lo: 2; x = x_hi * 2 + x_lo), y: 4, z: 4, core: 2. Of those that a mesh axis runs over, the one named last changes fastest.
Arguments:
- flux: bfloat16 [12288, 7808], P(('tmpl', 'spec', 'expo')), may hold values from -6 to 6
- ivar: bfloat16 [12288, 7808], P(('tmpl', 'spec', 'expo')), may hold values from 0.5 to 8
- pixel_mask: int32 [12288, 61], P(('tmpl', 'spec', 'expo')), may hold values 0 or 1
- exposure_target: int32 [12288], P(('tmpl', 'spec', 'expo')), may hold values from 0 to 63, as said below
- basis: bfloat16 [128, 10, 7808], P(('tmpl', 'spec')), may hold values from -0.0625 to 0.0625
- trial_counts: int32 [3], replicated, may hold values from 1 to 64, 128 in all
- target_class: int32 [4096], P(('tmpl', 'spec', 'expo')), may hold values from 0 to 2
Outputs:
- coefficients: float32 [10, 4096, 128], P(None, ('tmpl', 'spec', 'expo'))
- fit_gain: float32 [4096, 128], P(('tmpl', 'spec', 'expo'))
- best_gain: float32 [4096], P(('tmpl', 'spec', 'expo'))
The draws below stay inside these ranges and needn't reach their ends.
Inputs may be any that keep to these rules, and one draw needn't show every extreme that they name: `exposure_target`: every target of a group of 64 targets is named by at least one exposure of its group of 192 exposures. `trial_counts`: the counts sum to 128; class c takes the trials that follow those of the classes below it.
All inputs are finite; a program needn't handle non-finite values. No bound on the sum of `pixel_mask` on one device may be relied on, other than what follows from the above.
Results may differ from the reference program's by a relative error of at most 0.0038.
Values may be sent and summed in bfloat16 or wider, within the bound.
No kernel may reach another device: no remote copies, remote signals or barrier semaphores. Data moves between devices by JAX's collectives and lax.ppermute only.
A program may use at most 512 MiB of HBM per device.

```python
import math
import jax
import jax.numpy as jnp
import numpy as np
from jax import lax

P_SIZE = 7808
NBLK = 61
K = 10
CLASSES = 3
TGT_DEV = 32
EXP_DEV = 96
TARGETS = 4096
EXPOSURES = 12288
TRIALS = 128
N_EXPO = 2


def draw_exposure_target(key, part):
    key = jax.random.fold_in(key, 11)
    group_exposures = EXP_DEV * N_EXPO
    group_targets = TGT_DEV * N_EXPO
    group_count = EXPOSURES // group_exposures
    group_keys = jax.random.split(key, group_count)

    def per_group(group_key):
        first_key, second_key, third_key = jax.random.split(group_key, 3)
        covering = jax.random.permutation(first_key, group_targets)
        extras = jax.random.randint(second_key, (group_exposures - group_targets,), 0, group_targets)
        return jax.random.permutation(third_key, jnp.concatenate([covering, extras]))
    return jax.vmap(per_group)(group_keys).reshape(-1).astype(jnp.int32)


def touch_ends(values, stream_key, least, high):
    place = [jax.random.randint(jax.random.fold_in(stream_key, axis), (), 0, length) for axis, length in enumerate(values.shape)]
    widest = values.shape.index(max(values.shape))
    beside = place[:widest] + [(place[widest] + 1) % values.shape[widest]] + place[widest + 1:]
    return values.at[tuple(place)].set(least).at[tuple(beside)].set(high)


def steps_of(rng, shape, cuts, smallest, high):
    loudness = 1.0
    for dim, shards_of in cuts:
        steps = jax.random.uniform(jax.random.fold_in(jax.random.fold_in(rng, 6), dim), (shards_of,), jnp.float32, smallest / len(cuts), high / len(cuts))
        loudness = loudness * jnp.repeat(jnp.exp(steps), shape[dim] // shards_of).reshape((-1,) + (1,) * (len(shape) - 1 - dim))
    return loudness


def profile(number_of, total, reach, slope):
    weights = [(1 << 20) // math.isqrt(standing ** slope) + 1 for standing in range(2, number_of + 1)]
    surplus, holding = total - reach - (number_of - 1), [1] * (number_of - 1)
    while surplus > 0:
        candidates = [i for i in range(number_of - 1) if holding[i] < reach]
        pool, budget = sum([weights[i] for i in candidates]), surplus
        for i in candidates:
            more = min(reach - holding[i], max(1, budget * weights[i] // pool), surplus)
            holding[i] = holding[i] + more
            surplus = surplus - more
    return np.array([reach] + holding)


def ragged_sizes(own_key, amount, total, limit, skew):
    if amount == 2:
        one = jax.random.randint(own_key, (), max(1, total - limit), min(limit, total - 1) + 1)
        return jnp.stack([one, total - one])
    sizes = jnp.asarray(profile(amount, total, limit, skew), jnp.int32)
    couples = (amount - 1) // 2
    donor, receiver = sizes[1:1 + 2 * couples:2], sizes[2:2 + 2 * couples:2]
    margin = jnp.minimum(donor - 1, limit - receiver)
    passed = jax.random.randint(jax.random.fold_in(own_key, 1), (couples,), 0, 1 << 20) % (margin + 1)
    sizes = sizes.at[1:1 + 2 * couples:2].set(donor - passed).at[2:2 + 2 * couples:2].set(receiver + passed)
    return sizes[jax.random.permutation(jax.random.fold_in(own_key, 2), amount)]


def scatter_about(rng, shape, deviation, reach, pieces=(), kind=jnp.bfloat16):
    drawn = deviation * jax.random.normal(rng, shape, jnp.float32)
    if pieces:
        drawn = drawn * steps_of(rng, shape, pieces, -0.22, 0.18)
    return jnp.clip(drawn, -reach, reach).astype(kind)


def setup_inputs(seed: int = 0) -> dict:
    arg_keys = jax.random.split(jax.random.key(seed), 8)
    return {
        "flux": scatter_about(arg_keys[0], (EXPOSURES, P_SIZE), 1.0, 6.0, ((0, 128),)),
        "ivar": jnp.clip(jnp.exp(math.log(8.0) - 2.7725887 * jax.random.uniform(arg_keys[1], (EXPOSURES, P_SIZE), jnp.float32) ** steps_of(arg_keys[1], (EXPOSURES, P_SIZE), ((0, 128),), -0.2, 0.2)), 0.5, 8.0).astype(jnp.bfloat16),
        "pixel_mask": touch_ends((jax.random.randint(arg_keys[2], (EXPOSURES, NBLK), 0, 10) < 9).astype(jnp.int32), jax.random.fold_in(arg_keys[2], 1), 0, 1),
        "exposure_target": draw_exposure_target(jax.random.fold_in(arg_keys[7], 71), 0),
        "basis": scatter_about(arg_keys[4], (TRIALS, K, P_SIZE), P_SIZE ** -0.5, 0.0625, ((0, 64),)),
        "trial_counts": ragged_sizes(arg_keys[5], CLASSES, TRIALS, TRIALS // 2, 2).astype(jnp.int32),
        "target_class": touch_ends(jax.random.randint(arg_keys[6], (TARGETS,), 0, CLASSES), jax.random.fold_in(arg_keys[6], 1), 0, CLASSES - 1).astype(jnp.int32),
    }


def upper_pairs(term_count):
    leading = []
    trailing = []
    for upper_idx in range(term_count):
        for lower_idx in range(upper_idx, term_count):
            leading.append(upper_idx)
            trailing.append(lower_idx)
    return (np.array(leading), np.array(trailing))

def cholesky_solve(entries, right_side, term_count):
    lookup = {}
    position = 0
    for upper_idx in range(term_count):
        for lower_idx in range(upper_idx, term_count):
            lookup[upper_idx, lower_idx] = entries[position]
            lookup[lower_idx, upper_idx] = entries[position]
            position += 1
    factor = {}
    for column in range(term_count):
        partial_value = lookup[column, column]
        for earlier in range(column):
            partial_value = partial_value - factor[column, earlier] * factor[column, earlier]
        diag_root = jnp.sqrt(partial_value)
        factor[column, column] = diag_root
        for across in range(column + 1, term_count):
            partial_value = lookup[across, column]
            for earlier in range(column):
                partial_value = partial_value - factor[across, earlier] * factor[column, earlier]
            factor[across, column] = partial_value / diag_root
    forward = []
    for across in range(term_count):
        partial_value = right_side[across]
        for earlier in range(across):
            partial_value = partial_value - factor[across, earlier] * forward[earlier]
        forward.append(partial_value / factor[across, across])
    answer = [None] * term_count
    for across in reversed(range(term_count)):
        partial_value = forward[across]
        for earlier in range(across + 1, term_count):
            partial_value = partial_value - factor[earlier, across] * answer[earlier]
        answer[across] = partial_value / factor[across, across]
    return jnp.stack(answer)

def fit_block(coadd_ivar, coadd_wflux, trial_block):
    term_count = trial_block.shape[1]
    leading, trailing = upper_pairs(term_count)
    prior_diag = (leading == trailing).astype(np.float32)
    wide_block = trial_block.astype(jnp.float32)
    products = (wide_block[:, leading, :] * wide_block[:, trailing, :]).astype(jnp.bfloat16)
    normal = jnp.einsum('tp,gqp->qtg', coadd_ivar, products.astype(jnp.float32), precision=lax.Precision.HIGHEST)
    normal = normal + jnp.asarray(prior_diag, dtype=jnp.float32)[:, None, None]
    project = jnp.einsum('tp,gkp->ktg', coadd_wflux, wide_block, precision=lax.Precision.HIGHEST)
    coefs = cholesky_solve([normal[element] for element in range(normal.shape[0])], [project[element] for element in range(term_count)], term_count)
    gains = lax.optimization_barrier(jnp.sum(project * coefs, axis=0)) / term_count
    return (coefs, gains)

def reference(flux, ivar, pixel_mask, exposure_target, basis, trial_counts, target_class):
    rows_all = flux.shape[0]
    masked = ivar.reshape(rows_all, NBLK, P_SIZE // NBLK) * pixel_mask.astype(jnp.bfloat16)[:, :, None]
    weighted_ivar = masked.reshape(rows_all, P_SIZE)
    weighted_flux = (weighted_ivar.astype(jnp.float32) * flux.astype(jnp.float32)).astype(jnp.bfloat16)
    exposure_rows = jnp.arange(EXPOSURES, dtype=jnp.int32)
    owner = exposure_rows // (EXP_DEV * N_EXPO) * (TGT_DEV * N_EXPO) + exposure_target
    summed_flux = jax.ops.segment_sum(weighted_flux.astype(jnp.float32), owner, num_segments=TARGETS)
    summed_ivar = jax.ops.segment_sum(weighted_ivar.astype(jnp.float32), owner, num_segments=TARGETS)
    coadd_wflux = summed_flux.astype(jnp.bfloat16).astype(jnp.float32)
    coadd_ivar = summed_ivar.astype(jnp.bfloat16).astype(jnp.float32)
    grouped = basis.reshape(TRIALS // 8, 8, K, P_SIZE)
    coefs, gains = lax.map(lambda trial_block: fit_block(coadd_ivar, coadd_wflux, trial_block), grouped)
    coefficients = jnp.transpose(coefs, (1, 2, 0, 3)).reshape(K, TARGETS, TRIALS)
    gains = jnp.transpose(gains, (1, 0, 2)).reshape(TARGETS, TRIALS)
    class_ends = jnp.cumsum(trial_counts)
    trial_ids = jnp.arange(TRIALS, dtype=jnp.int32)
    trial_class = lax.optimization_barrier(jnp.sum((trial_ids[:, None] >= class_ends[None, :]).astype(jnp.int32), axis=1))
    valid = trial_class[None, :] == target_class[:, None]
    fit_gain = jnp.where(valid, gains, jnp.zeros_like(gains))
    best_gain = lax.optimization_barrier(jnp.max(fit_gain, axis=1))
    return (coefficients, fit_gain, best_gain)
```

```python
import jax
import jax.numpy as jnp
import numpy as np
from jax import lax
from jax.experimental import pallas as pl
from jax.experimental.pallas import tpu as pltpu
from jax.sharding import PartitionSpec as P

AXES = ("tmpl", "spec", "expo")
SIDES = (2, 4, 4, 2, 2)
TERMS = 10
HALVES = TERMS // 2
SLICES = 16
WIDTH = 512
COMBOS = 30
ROWS = COMBOS * 16 + TERMS * 8
VMEM = 56 * 1024 * 1024


def moved(device, core=0, x_lo=0, x_hi=0, along=None, step=0):
    h, z, y, lo, c = (int(v) for v in np.unravel_index(device, SIDES))
    if along is not None:
        if (c == 0) == (along == 0):
            z = (z + step) % 4
        else:
            y = (y + step) % 4
    return int(np.ravel_multi_index((h ^ x_hi, z, y, lo ^ x_lo, c ^ core), SIDES))


def send(value, **how):
    return lax.ppermute(value, AXES, [(d, moved(d, **how)) for d in range(128)])


def combos():
    out = [(m, n, 0) for m in range(HALVES) for n in range(m + 1, HALVES)]
    out += [(m, n, 1) for m in range(HALVES) for n in range(m + 1, HALVES)]
    out += [(m, m, 0) for m in range(HALVES)]
    out += [(m, m, 1) for m in range(HALVES)]
    return out


def entry_rows():
    where = {}
    for i, (m, n, crossed) in enumerate(combos()):
        for half in range(2):
            k, l = 2 * m + half, 2 * n + (half ^ crossed)
            where.setdefault((min(k, l), max(k, l)), i * 16 + half * 8)
    return where


def prep_kernel(place, basis, out, rows):
    core = place[0]
    pixels = basis.shape[2]
    rows[...] = jnp.zeros_like(rows)
    mine = jnp.where(core == 0, basis[0].astype(jnp.float32), basis[1].astype(jnp.float32))
    for h in range(SLICES):
        width = min(WIDTH, pixels - h * WIDTH)
        for k in range(TERMS):
            rows[k * SLICES + h : k * SLICES + h + 1, :width] = mine[k : k + 1, h * WIDTH : h * WIDTH + width]
    out[...] = rows[...].astype(jnp.bfloat16).reshape(out.shape)


def weight_kernel(flux, ivar, mask, owner, out):
    step = pl.program_id(0)

    @pl.when(step < pl.num_programs(0) - 1)
    def _():
        good = mask[...].astype(jnp.float32)
        for b in range(good.shape[1]):
            lanes = slice(b * 128, (b + 1) * 128)
            masked = (ivar[:, lanes].astype(jnp.float32) * good[:, b : b + 1]).astype(jnp.bfloat16)
            out[0, 0:16, lanes] = masked
            out[0, 16:32, lanes] = (masked.astype(jnp.float32) * flux[:, lanes].astype(jnp.float32)).astype(jnp.bfloat16)

    @pl.when(step == pl.num_programs(0) - 1)
    def _():
        out[...] = jnp.zeros_like(out)
        names = owner[...].astype(jnp.float32)
        out[0, 0:16, 0 : names.shape[1]] = jnp.broadcast_to(names, (16, names.shape[1])).astype(jnp.bfloat16)


def coadd_kernel(place, own_names, other_names, own, other, coadd_ivar, coadd_wflux, outgoing):
    core = place[0]
    row = lax.broadcasted_iota(jnp.int32, (64, 96), 0)
    wanted = jnp.where(row < 32, row + core * 32, row - core * 32).astype(jnp.float32)
    sums = []
    for part in range(2):
        total = None
        for names, block in ((own_names, own), (other_names, other)):
            select = (names[0, 0:1, 0:96].astype(jnp.float32) == wanted).astype(jnp.bfloat16)
            spectra = block[0:6, part * 16 : part * 16 + 16, :].reshape(96, block.shape[2])
            piece = jnp.dot(select, spectra, preferred_element_type=jnp.float32)
            total = piece if total is None else total + piece
        sums.append(total)
    coadd_ivar[...] = sums[0].astype(jnp.bfloat16)
    coadd_wflux[...] = sums[1].astype(jnp.bfloat16)
    outgoing[...] = jnp.where(core == 0, sums[0], sums[1]).astype(jnp.bfloat16)


def solve(entries, right):
    lower, scaled, inverse = {}, {}, []
    for j in range(TERMS):
        pivot = entries[j, j]
        for e in range(j):
            pivot = pivot - lower[j, e] * scaled[j, e]
        inverse.append(1.0 / pivot)
        for i in range(j + 1, TERMS):
            value = entries[j, i]
            for e in range(j):
                value = value - lower[i, e] * scaled[j, e]
            scaled[i, j] = value
            lower[i, j] = value * inverse[j]
    forward = []
    for i in range(TERMS):
        value = right[i]
        for e in range(i):
            value = value - lower[i, e] * forward[e]
        forward.append(value)
    answer = [None] * TERMS
    for i in reversed(range(TERMS)):
        value = forward[i] * inverse[i]
        for e in range(i + 1, TERMS):
            value = value - lower[e, i] * answer[e]
        answer[i] = value
    return answer


def fit_blocks(core, parts_of_blocks, own_ivar, own_wflux, direct, swapped, even, odd, total):
    count = len(parts_of_blocks)
    pixels = own_ivar.shape[1]
    side = SLICES * 16
    row = lax.broadcasted_iota(jnp.int32, (side, side), 0)
    col = lax.broadcasted_iota(jnp.int32, (side, side), 1)
    same = ((row // 16) == (col % 16)) & ((row % 8) == (col // 32))
    half, source = (row // 8) % 2, (col // 16) % 2
    straight = (same & (half == source)).astype(jnp.float32).astype(jnp.bfloat16)
    crossed = (same & (half != source)).astype(jnp.float32).astype(jnp.bfloat16)
    for b, parts in enumerate(parts_of_blocks):
        for m in range(HALVES):
            pieces = [p[:, 2 * m : 2 * m + 2].reshape(p.shape[0] * 2 * SLICES, WIDTH) for p in parts]
            block = pieces[0] if len(pieces) == 1 else jnp.concatenate(pieces, axis=0)
            even[b, m] = jnp.dot(straight, block, preferred_element_type=jnp.float32).astype(jnp.bfloat16)
            odd[b, m] = jnp.dot(crossed, block, preferred_element_type=jnp.float32).astype(jnp.bfloat16)

    contract = (((1,), (1,)), ((), ()))

    def one_slice(h, width, first):
        start = h * WIDTH if isinstance(h, int) else pl.multiple_of(h * WIDTH, WIDTH)
        lanes = pl.ds(start, width)
        near = direct[:, lanes].astype(jnp.float32)
        far = jnp.concatenate([swapped[32:64, lanes], swapped[0:32, lanes]], axis=0).astype(jnp.float32)
        ivar_part = jnp.where(core == 0, near, far).astype(jnp.bfloat16)
        wflux_part = jnp.where(core == 0, far, near).astype(jnp.bfloat16)
        ivar = jnp.concatenate([own_ivar[:, lanes], ivar_part], axis=0)
        wflux = jnp.concatenate([own_wflux[:, lanes], wflux_part], axis=0)
        rows = pl.ds(h * 16 if isinstance(h, int) else pl.multiple_of(h * 16, 16), 16)
        for b in range(count):
            evens = [even[b, m, rows, 0:width] for m in range(HALVES)]
            odds = [odd[b, m, rows, 0:width] for m in range(HALVES)]
            products = jnp.concatenate(
                [evens[m] * (odds[n] if cross else evens[n]) for m, n, cross in combos()], axis=0
            )
            normal = lax.dot_general(products, ivar, contract, preferred_element_type=jnp.float32)
            project = lax.dot_general(
                jnp.concatenate(evens, axis=0), wflux, contract, preferred_element_type=jnp.float32
            )
            if first:
                total[b, 0 : COMBOS * 16] = normal
                total[b, COMBOS * 16 : ROWS] = project
            else:
                total[b, 0 : COMBOS * 16] += normal
                total[b, COMBOS * 16 : ROWS] += project

    full = pixels // WIDTH
    one_slice(0, WIDTH, True)

    def step(h, carry):
        one_slice(h, WIDTH, False)
        return carry

    lax.fori_loop(1, full, step, 0)
    if pixels > full * WIDTH:
        one_slice(full, pixels - full * WIDTH, False)

    entries = {}
    for (k, l), at in entry_rows().items():
        value = total[:, at : at + 8, :]
        entries[k, l] = value + 1.0 if k == l else value
    right = [total[:, COMBOS * 16 + k * 8 : COMBOS * 16 + k * 8 + 8, :] for k in range(TERMS)]
    answer = solve(entries, right)
    gain = right[0] * answer[0]
    for k in range(1, TERMS):
        gain = gain + right[k] * answer[k]
    values = answer + [gain / TERMS, jnp.zeros_like(gain)]
    lane = lax.broadcasted_iota(jnp.int32, values[0].shape, 2) // 32
    packed = []
    for group in range(4):
        packed.append([])
        for q in range(3):
            out = None
            for k in range(4):
                shift = (k - group) % 4 * 32
                value = values[4 * q + k]
                value = pltpu.roll(value, shift, 2) if shift else value
                out = value if out is None else jnp.where(lane == k, value, out)
            packed[-1].append(out)
    return packed


def first_fit_kernel(place, own, up, down, own_ivar, own_wflux, direct, swapped, out, even, odd, total):
    packed = fit_blocks(place[0], [[own], [up], [down]], own_ivar, own_wflux, direct, swapped, even, odd, total)
    for group in range(4):
        for q in range(3):
            out[group, :, q] = packed[group][q]


def last_fit_kernel(place, first, far_a, far_b, own_ivar, own_wflux, direct, swapped, *rest):
    outs, (even, odd, total) = rest[:4], rest[4:]
    packed = fit_blocks(place[0], [[far_a, far_b]], own_ivar, own_wflux, direct, swapped, even, odd, total)
    for group in range(4):
        outs[group][0:3] = first[group]
        for q in range(3):
            outs[group][3:4, q] = packed[group][q]


def final_kernel(place, counts, classes, part_0, part_1, part_2, part_3, coefs, gains, best):
    core, lo, hi, z, y = (place[i] for i in range(5))

    def shift(n):
        return jnp.where(n == 1, 3, jnp.where(n == 2, 1, jnp.where(n == 3, 2, 0)))

    def trial_of(i):
        group, b, t = i // 32, (i // 8) % 4, i % 8
        source_core = core ^ (group % 2)
        source_lo = lo ^ (group // 2)
        near, far = shift(t // 2), shift(b)
        z_of = (z + jnp.where(source_core == 0, near, far)) % 4
        y_of = (y + jnp.where(source_core == 0, far, near)) % 4
        return (hi ^ (t % 2)) * 64 + z_of * 16 + y_of * 4 + source_lo * 2 + source_core

    trial = trial_of(lax.broadcasted_iota(jnp.int32, (128, 128), 0))
    lane = lax.broadcasted_iota(jnp.int32, (128, 128), 1)
    to_lane = (trial == lane).astype(jnp.float32)
    end_0 = counts[0]
    end_1 = end_0 + counts[1]
    end_2 = end_1 + counts[2]
    trial_class = sum((trial >= end).astype(jnp.int32) for end in (end_0, end_1, end_2))
    for q in range(3):
        rows = jnp.concatenate([p[:, q].reshape(32, 128) for p in (part_0, part_1, part_2, part_3)], axis=0)
        if q == 2:
            drop = (lane // 32 == 2) & (trial_class != classes[...])
            rows = jnp.where(drop, 0.0, rows)
            best[...] = jnp.max(rows, axis=0, keepdims=True)[:, 64:96]
        turned = lax.dot_general(
            rows, to_lane, (((0,), (0,)), ((), ())), precision=lax.Precision.HIGHEST, preferred_element_type=jnp.float32
        )
        for k in range(4):
            if 4 * q + k < TERMS:
                coefs[4 * q + k] = turned[k * 32 : (k + 1) * 32]
            elif 4 * q + k == TERMS:
                gains[...] = turned[k * 32 : (k + 1) * 32]


def body(flux, ivar, pixel_mask, exposure_target, basis, trial_counts, target_class):
    pixels = flux.shape[1]
    tmpl, spec, core = (lax.axis_index(a) for a in AXES)
    place = jnp.stack([core, spec % 2, tmpl // 4, tmpl % 4, spec // 2]).astype(jnp.int32)
    smem = pl.BlockSpec(memory_space=pltpu.SMEM)
    vmem = pl.BlockSpec(memory_space=pltpu.VMEM)
    params = pltpu.CompilerParams(vmem_limit_bytes=VMEM)

    trial = pl.pallas_call(
        prep_kernel,
        out_shape=jax.ShapeDtypeStruct((1, TERMS, SLICES, WIDTH), jnp.bfloat16),
        in_specs=[smem, vmem],
        out_specs=vmem,
        scratch_shapes=[pltpu.VMEM((TERMS * SLICES, WIDTH), jnp.float32)],
        compiler_params=params,
        name="prep",
    )(place, basis)
    pair = jnp.concatenate([trial, send(trial, x_hi=1)], axis=0)

    blocks = flux.shape[0] // 16
    weighted = pl.pallas_call(
        weight_kernel,
        out_shape=jax.ShapeDtypeStruct((blocks + 1, 32, pixels), jnp.bfloat16),
        grid=(blocks + 1,),
        in_specs=[
            pl.BlockSpec((16, pixels), lambda i: (jnp.minimum(i, blocks - 1), 0)),
            pl.BlockSpec((16, pixels), lambda i: (jnp.minimum(i, blocks - 1), 0)),
            pl.BlockSpec((16, pixel_mask.shape[1]), lambda i: (jnp.minimum(i, blocks - 1), 0)),
            pl.BlockSpec((1, flux.shape[0]), lambda i: (0, 0)),
        ],
        out_specs=pl.BlockSpec((1, 32, pixels), lambda i: (i, 0, 0)),
        compiler_params=params,
        name="weight",
    )(flux, ivar, pixel_mask, exposure_target.reshape(1, -1))
    weighted_other = send(weighted, core=1)

    eight = jnp.concatenate([pair] + [send(pair, along=0, step=s) for s in (1, -1, 2)], axis=0)

    chunk = 1024
    names = pl.BlockSpec((1, 16, 128), lambda i: (blocks, 0, 0))
    spectra = pl.BlockSpec((blocks + 1, 32, chunk), lambda i: (0, 0, i))
    coadd = pl.BlockSpec((64, chunk), lambda i: (0, i))
    coadd_shape = jax.ShapeDtypeStruct((64, pixels), jnp.bfloat16)
    own_ivar, own_wflux, outgoing = pl.pallas_call(
        coadd_kernel,
        out_shape=(coadd_shape,) * 3,
        grid=(pl.cdiv(pixels, chunk),),
        in_specs=[smem, names, names, spectra, spectra],
        out_specs=(coadd,) * 3,
        compiler_params=params,
        name="coadd",
    )(place, weighted, weighted_other, weighted, weighted_other)
    direct = send(outgoing, x_lo=1)
    swapped = send(direct, core=1)

    up, down = (send(eight, along=1, step=s) for s in (1, -1))
    far_a = send(up[:4], along=1, step=1)
    far_b = send(down[4:], along=1, step=-1)

    def fit_scratch(count):
        return [
            pltpu.VMEM((count, HALVES, 16 * SLICES, WIDTH), jnp.bfloat16),
            pltpu.VMEM((count, HALVES, 16 * SLICES, WIDTH), jnp.bfloat16),
            pltpu.VMEM((count, ROWS, 128), jnp.float32),
        ]

    first = pl.pallas_call(
        first_fit_kernel,
        out_shape=jax.ShapeDtypeStruct((4, 3, 3, 8, 128), jnp.float32),
        in_specs=[smem] + [vmem] * 7,
        out_specs=vmem,
        scratch_shapes=fit_scratch(3),
        compiler_params=params,
        name="first_fit",
    )(place, eight, up, down, own_ivar, own_wflux, direct, swapped)
    parts = pl.pallas_call(
        last_fit_kernel,
        out_shape=(jax.ShapeDtypeStruct((4, 3, 8, 128), jnp.float32),) * 4,
        in_specs=[smem] + [vmem] * 7,
        out_specs=(vmem,) * 4,
        scratch_shapes=fit_scratch(1),
        compiler_params=params,
        name="last_fit",
    )(place, first, far_a, far_b, own_ivar, own_wflux, direct, swapped)

    parts = (
        parts[0],
        send(parts[1], core=1),
        send(parts[2], x_lo=1),
        send(parts[3], x_lo=1, core=1),
    )
    coefs, gains, best = pl.pallas_call(
        final_kernel,
        out_shape=(
            jax.ShapeDtypeStruct((TERMS, 32, 128), jnp.float32),
            jax.ShapeDtypeStruct((32, 128), jnp.float32),
            jax.ShapeDtypeStruct((1, 32), jnp.float32),
        ),
        in_specs=[smem, smem] + [vmem] * 5,
        out_specs=(vmem,) * 3,
        compiler_params=params,
        name="final",
    )(place, trial_counts, jnp.tile(target_class, 4).reshape(1, 128), *parts)
    return coefs, gains, best.reshape(32)


def solution(mesh):
    rows = P(AXES, None)
    return jax.shard_map(
        body,
        mesh=mesh,
        in_specs=(rows, rows, rows, P(AXES), P(("tmpl", "spec"), None, None), P(), P(AXES)),
        out_specs=(P(None, AXES, None), P(AXES, None), P(AXES)),
        check_vma=False,
    )
```

```python
import jax
import jax.numpy as jnp
import numpy as np
from jax import lax
from jax.experimental import pallas as pl
from jax.experimental.pallas import tpu as pltpu
from jax.sharding import PartitionSpec as P

AXES = ("tmpl", "spec", "expo")
SIDES = (2, 4, 4, 2, 2)
TERMS = 10
HALVES = TERMS // 2
SLICES = 16
WIDTH = 512
COMBOS = 30
ROWS = COMBOS * 16 + TERMS * 8
VMEM = 24 * 1024 * 1024


def moved(device, core=0, x_lo=0, x_hi=0, along=None, step=0):
    h, z, y, lo, c = (int(v) for v in np.unravel_index(device, SIDES))
    if along is not None:
        if (c == 0) == (along == 0):
            z = (z + step) % 4
        else:
            y = (y + step) % 4
    return int(np.ravel_multi_index((h ^ x_hi, z, y, lo ^ x_lo, c ^ core), SIDES))


def send(value, **how):
    return lax.ppermute(value, AXES, [(d, moved(d, **how)) for d in range(128)])


def combos():
    out = [(m, n, 0) for m in range(HALVES) for n in range(m + 1, HALVES)]
    out += [(m, n, 1) for m in range(HALVES) for n in range(m + 1, HALVES)]
    out += [(m, m, 0) for m in range(HALVES)]
    out += [(m, m, 1) for m in range(HALVES)]
    return out


def entry_rows():
    where = {}
    for i, (m, n, crossed) in enumerate(combos()):
        for half in range(2):
            k, l = 2 * m + half, 2 * n + (half ^ crossed)
            where.setdefault((min(k, l), max(k, l)), i * 16 + half * 8)
    return where


def prep_kernel(place, basis, out, rows):
    core = place[0]
    pixels = basis.shape[2]
    tail = pixels - (SLICES - 1) * WIDTH
    rows[...] = jnp.zeros_like(rows)
    for k in range(TERMS):
        both = basis[k].astype(jnp.float32)
        mine = jnp.where(core == 0, both[0:1], both[1:2])
        for h in range(SLICES):
            width = WIDTH if h < SLICES - 1 else tail
            rows[k * SLICES + h : k * SLICES + h + 1, :width] = mine[:, h * WIDTH : h * WIDTH + width]
    out[...] = rows[...].astype(jnp.bfloat16).reshape(out.shape)


def weight_kernel(place, flux, ivar, mask, owner, keep, out, good):
    step, steps = pl.program_id(0), pl.num_programs(0)
    core = place[0]
    height = flux.shape[0]

    @pl.when(step == 0)
    def _():
        good[...] = mask[...].astype(jnp.float32).T

    @pl.when(step < steps - 1)
    def _():
        flags = good[pl.ds(pl.multiple_of(step * height, height), height), :]
        for b in range(flags.shape[1]):
            lanes = slice(b * 128, (b + 1) * 128)
            flag = jnp.broadcast_to(flags[:, b : b + 1], (height, 128)).astype(jnp.bfloat16)
            masked = ivar[:, lanes] * flag
            wide = masked.astype(jnp.float32)
            fluxes = wide * flux[:, lanes].astype(jnp.float32)
            keep[:, lanes] = jnp.where(core == 0, wide, fluxes).astype(jnp.bfloat16)
            out[:, lanes] = jnp.where(core == 0, fluxes, wide).astype(jnp.bfloat16)

    @pl.when(step == steps - 1)
    def _():
        names = owner[...].astype(jnp.float32)
        out[0:16, :] = jnp.zeros((16, out.shape[1]), jnp.bfloat16)
        out[0:16, 0 : names.shape[1]] = jnp.broadcast_to(names, (16, names.shape[1])).astype(jnp.bfloat16)


def coadd_kernel(place, own_names, other_names, own, other, coadd):
    core = place[0]
    count = own.shape[0]
    row = lax.broadcasted_iota(jnp.int32, (64, count), 0)
    wanted = jnp.where(row < 32, row + core * 32, row - core * 32).astype(jnp.float32)
    near = (own_names[...].astype(jnp.float32) == wanted).astype(jnp.float32)
    far = (other_names[0:1, 0:count].astype(jnp.float32) == wanted).astype(jnp.float32)
    select = jnp.concatenate([near, far], axis=1).astype(jnp.bfloat16)
    spectra = jnp.concatenate([own[...], other[...]], axis=0)
    coadd[...] = jnp.dot(select, spectra, preferred_element_type=jnp.float32).astype(jnp.bfloat16)


def join_kernel(own, up, down, far, out):
    side = SLICES * 16
    row = lax.broadcasted_iota(jnp.int32, (side, side), 0)
    col = lax.broadcasted_iota(jnp.int32, (side, side), 1)
    same = ((row // 16) == (col % 16)) & ((row % 8) == (col // 32)) & ((row // 8) % 2 == (col // 16) % 2)
    order = same.astype(jnp.float32).astype(jnp.bfloat16)
    for m in range(HALVES):
        block = jnp.concatenate(
            [p[:, 2 * m : 2 * m + 2].reshape(p.shape[0] * 2 * SLICES, WIDTH) for p in (own, up, down, far)], axis=0
        )
        turned = jnp.dot(order, block, preferred_element_type=jnp.float32).astype(jnp.bfloat16)
        out[:, m] = turned.reshape(SLICES, 16, WIDTH)


def solve(entries, right):
    lower, scaled, inverse = {}, {}, []
    for j in range(TERMS):
        pivot = entries[j, j]
        for e in range(j):
            pivot = pivot - lower[j, e] * scaled[j, e]
        inverse.append(1.0 / pivot)
        for i in range(j + 1, TERMS):
            value = entries[j, i]
            for e in range(j):
                value = value - lower[i, e] * scaled[j, e]
            scaled[i, j] = value
            lower[i, j] = value * inverse[j]
    forward = []
    for i in range(TERMS):
        value = right[i]
        for e in range(i):
            value = value - lower[i, e] * forward[e]
        forward.append(value)
    answer = [None] * TERMS
    for i in reversed(range(TERMS)):
        value = forward[i] * inverse[i]
        for e in range(i + 1, TERMS):
            value = value - lower[e, i] * answer[e]
        answer[i] = value
    return answer


def fit_blocks(core, blocks, mine, direct, over, swapped, total):
    pixels = mine.shape[1]
    contract = (((1,), (1,)), ((), ()))

    def one_slice(h, segment, at, width, first):
        static = isinstance(h, int)
        lanes = pl.ds(h * WIDTH if static else pl.multiple_of(h * WIDTH, WIDTH), width)
        near = jnp.concatenate([mine[:, lanes], direct[:, lanes]], axis=0)
        far = jnp.concatenate(
            [over[32:64, lanes], over[0:32, lanes], swapped[32:64, lanes], swapped[0:32, lanes]], axis=0
        )
        ivar = jnp.where(core == 0, near, far)
        wflux = jnp.where(core == 0, far, near)
        for b, refs in enumerate(blocks):
            evens = [refs[segment][at, m, :, 0:width] for m in range(HALVES)]
            odds = [jnp.concatenate([e[8:16], e[0:8]], axis=0) for e in evens]
            products = jnp.concatenate(
                [evens[m] * (odds[n] if cross else evens[n]) for m, n, cross in combos()], axis=0
            )
            normal = lax.dot_general(products, ivar, contract, preferred_element_type=jnp.float32)
            project = lax.dot_general(
                jnp.concatenate(evens, axis=0), wflux, contract, preferred_element_type=jnp.float32
            )
            if first:
                total[b, 0 : COMBOS * 16] = normal
                total[b, COMBOS * 16 : ROWS] = project
            else:
                total[b, 0 : COMBOS * 16] += normal
                total[b, COMBOS * 16 : ROWS] += project

    full = pixels // WIDTH
    segments = len(blocks[0])
    per = SLICES // segments
    one_slice(0, 0, 0, WIDTH, True)
    for segment in range(segments):

        def step(h, carry, segment=segment):
            one_slice(h, segment, h - segment * per, WIDTH, False)
            return carry

        lax.fori_loop(max(1, segment * per), min(full, (segment + 1) * per), step, 0)
    if pixels > full * WIDTH:
        one_slice(full, full // per, full % per, pixels - full * WIDTH, False)

    entries = {}
    for (k, l), at in entry_rows().items():
        value = total[:, at : at + 8, :]
        entries[k, l] = value + 1.0 if k == l else value
    right = [total[:, COMBOS * 16 + k * 8 : COMBOS * 16 + k * 8 + 8, :] for k in range(TERMS)]
    answer = solve(entries, right)
    gain = right[0] * answer[0]
    for k in range(1, TERMS):
        gain = gain + right[k] * answer[k]
    values = answer + [gain / TERMS, jnp.zeros_like(gain)]
    lane = lax.broadcasted_iota(jnp.int32, values[0].shape, 2) // 32
    packed = []
    for group in range(4):
        packed.append([])
        for q in range(3):
            out = None
            for k in range(4):
                shift = (k - group) % 4 * 32
                value = values[4 * q + k]
                value = pltpu.roll(value, shift, 2) if shift else value
                out = value if out is None else jnp.where(lane == k, value, out)
            packed[-1].append(out)
    return packed


def first_fit_kernel(place, own, up, down, mine, direct, over, swapped, out, total):
    packed = fit_blocks(place[0], [[own], [up], [down]], mine, direct, over, swapped, total)
    for group in range(4):
        for q in range(3):
            out[group, :, q] = packed[group][q]


def last_fit_kernel(place, first, far_a, far_b, mine, direct, over, swapped, *rest):
    outs, total = rest[:4], rest[4]
    packed = fit_blocks(place[0], [[far_a, far_b]], mine, direct, over, swapped, total)
    for group in range(4):
        outs[group][0:3] = first[group]
        for q in range(3):
            outs[group][3:4, q] = packed[group][q]


def final_kernel(place, counts, classes, part_0, part_1, part_2, part_3, coefs, gains, best):
    core, lo, hi, z, y = (place[i] for i in range(5))

    def shift(n):
        return jnp.where(n == 1, 3, jnp.where(n == 2, 1, jnp.where(n == 3, 2, 0)))

    def trial_of(i):
        group, b, t = i // 32, (i // 8) % 4, i % 8
        source_core = core ^ (group % 2)
        source_lo = lo ^ (group // 2)
        near, far = shift(t // 2), shift(b)
        z_of = (z + jnp.where(source_core == 0, near, far)) % 4
        y_of = (y + jnp.where(source_core == 0, far, near)) % 4
        return (hi ^ (t % 2)) * 64 + z_of * 16 + y_of * 4 + source_lo * 2 + source_core

    trial = trial_of(lax.broadcasted_iota(jnp.int32, (128, 128), 0))
    lane = lax.broadcasted_iota(jnp.int32, (128, 128), 1)
    to_lane = (trial == lane).astype(jnp.float32)
    end_0 = counts[0]
    end_1 = end_0 + counts[1]
    end_2 = end_1 + counts[2]
    trial_class = sum((trial >= end).astype(jnp.int32) for end in (end_0, end_1, end_2))
    for q in range(3):
        rows = jnp.concatenate([p[:, q].reshape(32, 128) for p in (part_0, part_1, part_2, part_3)], axis=0)
        if q == 2:
            drop = (lane // 32 == 2) & (trial_class != classes[...])
            rows = jnp.where(drop, 0.0, rows)
            best[...] = jnp.max(rows, axis=0, keepdims=True)[:, 64:96]
        turned = lax.dot_general(
            rows, to_lane, (((0,), (0,)), ((), ())), precision=lax.Precision.HIGHEST, preferred_element_type=jnp.float32
        )
        for k in range(4):
            if 4 * q + k < TERMS:
                coefs[4 * q + k] = turned[k * 32 : (k + 1) * 32]
            elif 4 * q + k == TERMS:
                gains[...] = turned[k * 32 : (k + 1) * 32]


def body(flux, ivar, pixel_mask, exposure_target, basis, trial_counts, target_class):
    pixels = flux.shape[1]
    tmpl, spec, core = (lax.axis_index(a) for a in AXES)
    place = jnp.stack([core, spec % 2, tmpl // 4, tmpl % 4, spec // 2]).astype(jnp.int32)
    smem = pl.BlockSpec(memory_space=pltpu.SMEM)
    vmem = pl.BlockSpec(memory_space=pltpu.VMEM)
    params = pltpu.CompilerParams(vmem_limit_bytes=VMEM)

    trial = pl.pallas_call(
        prep_kernel,
        out_shape=jax.ShapeDtypeStruct((1, TERMS, SLICES, WIDTH), jnp.bfloat16),
        in_specs=[smem, vmem],
        out_specs=vmem,
        scratch_shapes=[pltpu.VMEM((TERMS * SLICES, WIDTH), jnp.float32)],
        compiler_params=params,
        name="prep",
    )(place, jnp.transpose(basis, (1, 0, 2)))
    pair = jnp.concatenate([trial, send(trial, x_hi=1)], axis=0)

    trial, flux = lax.optimization_barrier((trial, flux))
    count = flux.shape[0]
    height = 32
    steps = count // height
    spectra = pl.BlockSpec((height, pixels), lambda i: (jnp.minimum(i, steps - 1), 0))
    owners = exposure_target.reshape(1, count)
    keep, outgoing = pl.pallas_call(
        weight_kernel,
        out_shape=(
            jax.ShapeDtypeStruct((count, pixels), jnp.bfloat16),
            jax.ShapeDtypeStruct((count + 16, pixels), jnp.bfloat16),
        ),
        grid=(steps + 1,),
        in_specs=[
            smem,
            spectra,
            spectra,
            pl.BlockSpec((pixel_mask.shape[1], count), lambda i: (0, 0)),
            pl.BlockSpec((1, count), lambda i: (0, 0)),
        ],
        out_specs=(spectra, pl.BlockSpec((height, pixels), lambda i: (i, 0))),
        scratch_shapes=[pltpu.VMEM((count, pixel_mask.shape[1]), jnp.float32)],
        compiler_params=params,
        name="weight",
    )(place, flux, ivar, pixel_mask.T, owners)
    incoming = send(outgoing, core=1)

    near = [pair] + [send(pair, along=0, step=s) for s in (1, -1, 2)]

    chunk = 2048
    rows = pl.BlockSpec((count, chunk), lambda i: (0, i))
    mine = pl.pallas_call(
        coadd_kernel,
        out_shape=jax.ShapeDtypeStruct((64, pixels), jnp.bfloat16),
        grid=(pl.cdiv(pixels, chunk),),
        in_specs=[
            smem,
            pl.BlockSpec((1, count), lambda i: (0, 0)),
            pl.BlockSpec((16, 128), lambda i: (count // 16, 0)),
            rows,
            rows,
        ],
        out_specs=pl.BlockSpec((64, chunk), lambda i: (0, i)),
        compiler_params=params,
        name="coadd",
    )(place, owners, incoming, keep, incoming)
    direct = send(mine, x_lo=1)
    over = send(mine, core=1)
    swapped = send(direct, core=1)

    eight = pl.pallas_call(
        join_kernel,
        out_shape=jax.ShapeDtypeStruct((SLICES, HALVES, 16, WIDTH), jnp.bfloat16),
        in_specs=[vmem] * 4,
        out_specs=vmem,
        compiler_params=params,
        name="join",
    )(*near)
    up, down = (send(eight, along=1, step=s) for s in (1, -1))
    far_a = send(up[: SLICES // 2], along=1, step=1)
    far_b = send(down[SLICES // 2 :], along=1, step=-1)

    first = pl.pallas_call(
        first_fit_kernel,
        out_shape=jax.ShapeDtypeStruct((4, 3, 3, 8, 128), jnp.float32),
        in_specs=[smem] + [vmem] * 7,
        out_specs=vmem,
        scratch_shapes=[pltpu.VMEM((3, ROWS, 128), jnp.float32)],
        compiler_params=params,
        name="first_fit",
    )(place, eight, up, down, mine, direct, over, swapped)
    parts = pl.pallas_call(
        last_fit_kernel,
        out_shape=(jax.ShapeDtypeStruct((4, 3, 8, 128), jnp.float32),) * 4,
        in_specs=[smem] + [vmem] * 7,
        out_specs=(vmem,) * 4,
        scratch_shapes=[pltpu.VMEM((1, ROWS, 128), jnp.float32)],
        compiler_params=params,
        name="last_fit",
    )(place, first, far_a, far_b, mine, direct, over, swapped)

    parts = (
        parts[0],
        send(parts[1], core=1),
        send(parts[2], x_lo=1),
        send(parts[3], x_lo=1, core=1),
    )
    coefs, gains, best = pl.pallas_call(
        final_kernel,
        out_shape=(
            jax.ShapeDtypeStruct((TERMS, 32, 128), jnp.float32),
            jax.ShapeDtypeStruct((32, 128), jnp.float32),
            jax.ShapeDtypeStruct((1, 32), jnp.float32),
        ),
        in_specs=[smem, smem] + [vmem] * 5,
        out_specs=(vmem,) * 3,
        compiler_params=params,
        name="final",
    )(place, trial_counts, jnp.tile(target_class, 4).reshape(1, 128), *parts)
    return coefs, gains, best.reshape(32)


def solution(mesh):
    rows = P(AXES, None)
    return jax.shard_map(
        body,
        mesh=mesh,
        in_specs=(rows, rows, rows, P(AXES), P(("tmpl", "spec"), None, None), P(), P(AXES)),
        out_specs=(P(None, AXES, None), P(AXES, None), P(AXES)),
        check_vma=False,
    )
```

```python
import jax
import jax.numpy as jnp
import numpy as np
from jax import lax
from jax.experimental import pallas as pl
from jax.experimental.pallas import tpu as pltpu
from jax.sharding import PartitionSpec as P

AXES = ("tmpl", "spec", "expo")
SIDES = (2, 4, 4, 2, 2)
TERMS = 10
HALVES = TERMS // 2
SLICES = 16
WIDTH = 512
COMBOS = 30
ROWS = COMBOS * 16 + TERMS * 8
VMEM = 24 * 1024 * 1024


def moved(device, core=0, x_lo=0, x_hi=0, along=None, step=0):
    h, z, y, lo, c = (int(v) for v in np.unravel_index(device, SIDES))
    if along is not None:
        if (c == 0) == (along == 0):
            z = (z + step) % 4
        else:
            y = (y + step) % 4
    return int(np.ravel_multi_index((h ^ x_hi, z, y, lo ^ x_lo, c ^ core), SIDES))


def send(value, **how):
    return lax.ppermute(value, AXES, [(d, moved(d, **how)) for d in range(128)])


def combos():
    out = [(m, n, 0) for m in range(HALVES) for n in range(m + 1, HALVES)]
    out += [(m, n, 1) for m in range(HALVES) for n in range(m + 1, HALVES)]
    out += [(m, m, 0) for m in range(HALVES)]
    out += [(m, m, 1) for m in range(HALVES)]
    return out


def entry_rows():
    where = {}
    for i, (m, n, crossed) in enumerate(combos()):
        for half in range(2):
            k, l = 2 * m + half, 2 * n + (half ^ crossed)
            where.setdefault((min(k, l), max(k, l)), i * 16 + half * 8)
    return where


def prep_kernel(place, basis, out, rows):
    core = place[0]
    pixels = basis.shape[2]
    tail = pixels - (SLICES - 1) * WIDTH
    rows[...] = jnp.zeros_like(rows)
    for k in range(TERMS):
        both = basis[k].astype(jnp.float32)
        mine = jnp.where(core == 0, both[0:1], both[1:2])
        for h in range(SLICES):
            width = WIDTH if h < SLICES - 1 else tail
            rows[k * SLICES + h : k * SLICES + h + 1, :width] = mine[:, h * WIDTH : h * WIDTH + width]
    out[...] = rows[...].astype(jnp.bfloat16).reshape(out.shape)


def weight_kernel(place, flux, ivar, mask, owner, keep, out, good):
    step, steps = pl.program_id(0), pl.num_programs(0)
    core = place[0]
    height = flux.shape[0]

    @pl.when(step == 0)
    def _():
        good[...] = mask[...].astype(jnp.float32).T

    @pl.when(step < steps - 1)
    def _():
        flags = good[pl.ds(pl.multiple_of(step * height, height), height), :]
        for b in range(flags.shape[1]):
            lanes = slice(b * 128, (b + 1) * 128)
            flag = jnp.broadcast_to(flags[:, b : b + 1], (height, 128)).astype(jnp.bfloat16)
            masked = ivar[:, lanes] * flag
            wide = masked.astype(jnp.float32)
            fluxes = wide * flux[:, lanes].astype(jnp.float32)
            keep[:, lanes] = jnp.where(core == 0, wide, fluxes).astype(jnp.bfloat16)
            out[:, lanes] = jnp.where(core == 0, fluxes, wide).astype(jnp.bfloat16)

    @pl.when(step == steps - 1)
    def _():
        names = owner[...].astype(jnp.float32)
        out[0:16, :] = jnp.zeros((16, out.shape[1]), jnp.bfloat16)
        out[0:16, 0 : names.shape[1]] = jnp.broadcast_to(names, (16, names.shape[1])).astype(jnp.bfloat16)


def coadd_kernel(place, own_names, other_names, own, other, coadd):
    core = place[0]
    count = own.shape[0]
    row = lax.broadcasted_iota(jnp.int32, (64, count), 0)
    wanted = jnp.where(row < 32, row + core * 32, row - core * 32).astype(jnp.float32)
    near = (own_names[...].astype(jnp.float32) == wanted).astype(jnp.float32)
    far = (other_names[0:1, 0:count].astype(jnp.float32) == wanted).astype(jnp.float32)
    select = jnp.concatenate([near, far], axis=1).astype(jnp.bfloat16)
    spectra = jnp.concatenate([own[...], other[...]], axis=0)
    coadd[...] = jnp.dot(select, spectra, preferred_element_type=jnp.float32).astype(jnp.bfloat16)


def join_kernel(own, up, down, far, out):
    side = SLICES * 16
    row = lax.broadcasted_iota(jnp.int32, (side, side), 0)
    col = lax.broadcasted_iota(jnp.int32, (side, side), 1)
    same = ((row // 16) == (col % 16)) & ((row % 8) == (col // 32)) & ((row // 8) % 2 == (col // 16) % 2)
    order = same.astype(jnp.float32).astype(jnp.bfloat16)
    for m in range(HALVES):
        block = jnp.concatenate(
            [p[:, 2 * m : 2 * m + 2].reshape(p.shape[0] * 2 * SLICES, WIDTH) for p in (own, up, down, far)], axis=0
        )
        turned = jnp.dot(order, block, preferred_element_type=jnp.float32).astype(jnp.bfloat16)
        for block in range(out.shape[0]):
            h, at = block // 4, block % 4 * 128
            out[block, m] = turned[h * 16 : h * 16 + 16, at : at + 128]


def solve(entries, right):
    lower, scaled, inverse = {}, {}, []
    for j in range(TERMS):
        pivot = entries[j, j]
        for e in range(j):
            pivot = pivot - lower[j, e] * scaled[j, e]
        inverse.append(1.0 / pivot)
        for i in range(j + 1, TERMS):
            value = entries[j, i]
            for e in range(j):
                value = value - lower[i, e] * scaled[j, e]
            scaled[i, j] = value
            lower[i, j] = value * inverse[j]
    forward = []
    for i in range(TERMS):
        value = right[i]
        for e in range(i):
            value = value - lower[i, e] * forward[e]
        forward.append(value)
    answer = [None] * TERMS
    for i in reversed(range(TERMS)):
        value = forward[i] * inverse[i]
        for e in range(i + 1, TERMS):
            value = value - lower[e, i] * answer[e]
        answer[i] = value
    return answer


def fit_blocks(core, blocks, mine, direct, over, swapped, total):
    pixels = mine.shape[1]
    contract = (((1,), (1,)), ((), ()))

    for at in range(0, pixels // 128, WIDTH // 128):
        taken = range(at, min(at + WIDTH // 128, pixels // 128))
        lanes = pl.ds(at * 128, len(taken) * 128)
        near = jnp.concatenate([mine[:, lanes], direct[:, lanes]], axis=0)
        far = jnp.concatenate(
            [over[32:64, lanes], over[0:32, lanes], swapped[32:64, lanes], swapped[0:32, lanes]], axis=0
        )
        ivar = jnp.where(core == 0, near, far)
        wflux = jnp.where(core == 0, far, near)
        for b, refs in enumerate(blocks):
            evens = []
            for m in range(HALVES):
                pieces = [refs[0][t, m] if t < refs[0].shape[0] else refs[1][t - refs[0].shape[0], m] for t in taken]
                evens.append(jnp.concatenate(pieces, axis=1))
            odds = [jnp.concatenate([e[8:16], e[0:8]], axis=0) for e in evens]
            products = jnp.concatenate(
                [evens[m] * (odds[n] if cross else evens[n]) for m, n, cross in combos()], axis=0
            )
            normal = lax.dot_general(products, ivar, contract, preferred_element_type=jnp.float32)
            project = lax.dot_general(
                jnp.concatenate(evens, axis=0), wflux, contract, preferred_element_type=jnp.float32
            )
            if at == 0:
                total[b, 0 : COMBOS * 16] = normal
                total[b, COMBOS * 16 : ROWS] = project
            else:
                total[b, 0 : COMBOS * 16] += normal
                total[b, COMBOS * 16 : ROWS] += project

    entries = {}
    for (k, l), at in entry_rows().items():
        value = total[:, at : at + 8, :]
        entries[k, l] = value + 1.0 if k == l else value
    right = [total[:, COMBOS * 16 + k * 8 : COMBOS * 16 + k * 8 + 8, :] for k in range(TERMS)]
    answer = solve(entries, right)
    gain = right[0] * answer[0]
    for k in range(1, TERMS):
        gain = gain + right[k] * answer[k]
    values = answer + [gain / TERMS, jnp.zeros_like(gain)]
    lane = lax.broadcasted_iota(jnp.int32, values[0].shape, 2) // 32
    packed = []
    for group in range(4):
        packed.append([])
        for q in range(3):
            out = None
            for k in range(4):
                shift = (k - group) % 4 * 32
                value = values[4 * q + k]
                value = pltpu.roll(value, shift, 2) if shift else value
                out = value if out is None else jnp.where(lane == k, value, out)
            packed[-1].append(out)
    return packed


def first_fit_kernel(place, own, up, down, mine, direct, over, swapped, out, total):
    packed = fit_blocks(place[0], [[own], [up], [down]], mine, direct, over, swapped, total)
    for group in range(4):
        for q in range(3):
            out[group, :, q] = packed[group][q]


def last_fit_kernel(place, first, far_a, far_b, mine, direct, over, swapped, *rest):
    outs, total = rest[:4], rest[4]
    packed = fit_blocks(place[0], [[far_a, far_b]], mine, direct, over, swapped, total)
    for group in range(4):
        outs[group][0:3] = first[group]
        for q in range(3):
            outs[group][3:4, q] = packed[group][q]


def final_kernel(place, counts, classes, part_0, part_1, part_2, part_3, coefs, gains, best):
    core, lo, hi, z, y = (place[i] for i in range(5))

    def shift(n):
        return jnp.where(n == 1, 3, jnp.where(n == 2, 1, jnp.where(n == 3, 2, 0)))

    def trial_of(i):
        group, b, t = i // 32, (i // 8) % 4, i % 8
        source_core = core ^ (group % 2)
        source_lo = lo ^ (group // 2)
        near, far = shift(t // 2), shift(b)
        z_of = (z + jnp.where(source_core == 0, near, far)) % 4
        y_of = (y + jnp.where(source_core == 0, far, near)) % 4
        return (hi ^ (t % 2)) * 64 + z_of * 16 + y_of * 4 + source_lo * 2 + source_core

    trial = trial_of(lax.broadcasted_iota(jnp.int32, (128, 128), 0))
    lane = lax.broadcasted_iota(jnp.int32, (128, 128), 1)
    to_lane = (trial == lane).astype(jnp.float32)
    end_0 = counts[0]
    end_1 = end_0 + counts[1]
    end_2 = end_1 + counts[2]
    trial_class = sum((trial >= end).astype(jnp.int32) for end in (end_0, end_1, end_2))
    for q in range(3):
        rows = jnp.concatenate([p[:, q].reshape(32, 128) for p in (part_0, part_1, part_2, part_3)], axis=0)
        if q == 2:
            drop = (lane // 32 == 2) & (trial_class != classes[...])
            rows = jnp.where(drop, 0.0, rows)
            best[...] = jnp.max(rows, axis=0, keepdims=True)[:, 64:96]
        turned = lax.dot_general(
            rows, to_lane, (((0,), (0,)), ((), ())), precision=lax.Precision.HIGHEST, preferred_element_type=jnp.float32
        )
        for k in range(4):
            if 4 * q + k < TERMS:
                coefs[4 * q + k] = turned[k * 32 : (k + 1) * 32]
            elif 4 * q + k == TERMS:
                gains[...] = turned[k * 32 : (k + 1) * 32]


def cost(micros):
    return pl.CostEstimate(flops=0, bytes_accessed=int(micros * 3.0e6), transcendentals=0)


def body(flux, ivar, pixel_mask, exposure_target, basis, trial_counts, target_class):
    pixels = flux.shape[1]
    tmpl, spec, core = (lax.axis_index(a) for a in AXES)
    place = jnp.stack([core, spec % 2, tmpl // 4, tmpl % 4, spec // 2]).astype(jnp.int32)
    smem = pl.BlockSpec(memory_space=pltpu.SMEM)
    vmem = pl.BlockSpec(memory_space=pltpu.VMEM)
    params = pltpu.CompilerParams(vmem_limit_bytes=VMEM)

    trial = pl.pallas_call(
        prep_kernel,
        out_shape=jax.ShapeDtypeStruct((1, TERMS, SLICES, WIDTH), jnp.bfloat16),
        in_specs=[smem, vmem],
        out_specs=vmem,
        scratch_shapes=[pltpu.VMEM((TERMS * SLICES, WIDTH), jnp.float32)],
        compiler_params=params,
        cost_estimate=cost(0.7),
        name="prep",
    )(place, jnp.transpose(basis, (1, 0, 2)))
    other = send(trial, x_hi=1)
    pair = jnp.concatenate([trial, other], axis=0)

    count = flux.shape[0]
    height = 32
    steps = count // height
    spectra = pl.BlockSpec((height, pixels), lambda i: (jnp.minimum(i, steps - 1), 0))
    owners = exposure_target.reshape(1, count)
    keep, outgoing = pl.pallas_call(
        weight_kernel,
        out_shape=(
            jax.ShapeDtypeStruct((count, pixels), jnp.bfloat16),
            jax.ShapeDtypeStruct((count + 16, pixels), jnp.bfloat16),
        ),
        grid=(steps + 1,),
        in_specs=[
            smem,
            spectra,
            spectra,
            pl.BlockSpec((pixel_mask.shape[1], count), lambda i: (0, 0)),
            pl.BlockSpec((1, count), lambda i: (0, 0)),
        ],
        out_specs=(spectra, pl.BlockSpec((height, pixels), lambda i: (i, 0))),
        scratch_shapes=[pltpu.VMEM((count, pixel_mask.shape[1]), jnp.float32)],
        compiler_params=params,
        cost_estimate=cost(2.3),
        name="weight",
    )(place, flux, ivar, pixel_mask.T, owners)
    outgoing, _ = lax.optimization_barrier((outgoing, other))
    incoming = send(outgoing, core=1)

    chunk = 2048
    rows = pl.BlockSpec((count, chunk), lambda i: (0, i))
    mine = pl.pallas_call(
        coadd_kernel,
        out_shape=jax.ShapeDtypeStruct((64, pixels), jnp.bfloat16),
        grid=(pl.cdiv(pixels, chunk),),
        in_specs=[
            smem,
            pl.BlockSpec((1, count), lambda i: (0, 0)),
            pl.BlockSpec((16, 128), lambda i: (count // 16, 0)),
            rows,
            rows,
        ],
        out_specs=pl.BlockSpec((64, chunk), lambda i: (0, i)),
        compiler_params=params,
        cost_estimate=cost(2.4),
        name="coadd",
    )(place, owners, incoming, keep, incoming)
    direct = send(mine, x_lo=1)
    over = send(mine, core=1)
    swapped = send(direct, core=1)

    near = [pair] + [send(pair, along=0, step=s) for s in (1, -1, 2)]

    eight = pl.pallas_call(
        join_kernel,
        out_shape=jax.ShapeDtypeStruct((pixels // 128, HALVES, 16, 128), jnp.bfloat16),
        in_specs=[vmem] * 4,
        out_specs=vmem,
        compiler_params=params,
        cost_estimate=cost(0.5),
        name="join",
    )(*near)
    up, down = (send(eight, along=1, step=s) for s in (1, -1))
    cut = pixels // 256
    far_a = send(up[:cut], along=1, step=1)
    far_b = send(down[cut:], along=1, step=-1)

    first = pl.pallas_call(
        first_fit_kernel,
        out_shape=jax.ShapeDtypeStruct((4, 3, 3, 8, 128), jnp.float32),
        in_specs=[smem] + [vmem] * 7,
        out_specs=vmem,
        scratch_shapes=[pltpu.VMEM((3, ROWS, 128), jnp.float32)],
        compiler_params=params,
        cost_estimate=cost(12),
        name="first_fit",
    )(place, eight, up, down, mine, direct, over, swapped)
    parts = pl.pallas_call(
        last_fit_kernel,
        out_shape=(jax.ShapeDtypeStruct((4, 3, 8, 128), jnp.float32),) * 4,
        in_specs=[smem] + [vmem] * 7,
        out_specs=(vmem,) * 4,
        scratch_shapes=[pltpu.VMEM((1, ROWS, 128), jnp.float32)],
        compiler_params=params,
        cost_estimate=cost(6),
        name="last_fit",
    )(place, first, far_a, far_b, mine, direct, over, swapped)

    parts = (
        parts[0],
        send(parts[1], core=1),
        send(parts[2], x_lo=1),
        send(parts[3], x_lo=1, core=1),
    )
    coefs, gains, best = pl.pallas_call(
        final_kernel,
        out_shape=(
            jax.ShapeDtypeStruct((TERMS, 32, 128), jnp.float32),
            jax.ShapeDtypeStruct((32, 128), jnp.float32),
            jax.ShapeDtypeStruct((1, 32), jnp.float32),
        ),
        in_specs=[smem, smem] + [vmem] * 5,
        out_specs=(vmem,) * 3,
        compiler_params=params,
        cost_estimate=cost(2),
        name="final",
    )(place, trial_counts, jnp.tile(target_class, 4).reshape(1, 128), *parts)
    return coefs, gains, best.reshape(32)


def solution(mesh):
    rows = P(AXES, None)
    return jax.shard_map(
        body,
        mesh=mesh,
        in_specs=(rows, rows, rows, P(AXES), P(("tmpl", "spec"), None, None), P(), P(AXES)),
        out_specs=(P(None, AXES, None), P(AXES, None), P(AXES)),
        check_vma=False,
    )
```

```python
import jax
import jax.numpy as jnp
import numpy as np
from jax import lax
from jax.experimental import pallas as pl
from jax.experimental.pallas import tpu as pltpu
from jax.sharding import PartitionSpec as P

AXES = ("tmpl", "spec", "expo")
SIDES = (2, 4, 4, 2, 2)
TERMS = 10
HALVES = TERMS // 2
SLICES = 16
WIDTH = 512
COMBOS = 30
ROWS = COMBOS * 16 + TERMS * 8
VMEM = 24 * 1024 * 1024


def moved(device, core=0, x_hi=0, x=0, along=None, step=0):
    h, z, y, lo, c = (int(v) for v in np.unravel_index(device, SIDES))
    if along is not None:
        if (c == 0) == (along == 0):
            z = (z + step) % 4
        else:
            y = (y + step) % 4
    h, lo = divmod((2 * h + lo + (x if c == 0 else -x)) % 4, 2)
    return int(np.ravel_multi_index((h ^ x_hi, z, y, lo, c ^ core), SIDES))


def send(value, **how):
    return lax.ppermute(value, AXES, [(d, moved(d, **how)) for d in range(128)])


def combos():
    out = [(m, n, 0) for m in range(HALVES) for n in range(m + 1, HALVES)]
    out += [(m, n, 1) for m in range(HALVES) for n in range(m + 1, HALVES)]
    out += [(m, m, 0) for m in range(HALVES)]
    out += [(m, m, 1) for m in range(HALVES)]
    return out


def entry_rows():
    where = {}
    for i, (m, n, crossed) in enumerate(combos()):
        for half in range(2):
            k, l = 2 * m + half, 2 * n + (half ^ crossed)
            where.setdefault((min(k, l), max(k, l)), i * 16 + half * 8)
    return where


def prep_kernel(place, basis, out, rows):
    core = place[0]
    pixels = basis.shape[2]
    tail = pixels - (SLICES - 1) * WIDTH
    rows[...] = jnp.zeros_like(rows)
    for k in range(TERMS):
        both = basis[k].astype(jnp.float32)
        mine = jnp.where(core == 0, both[0:1], both[1:2])
        for h in range(SLICES):
            width = WIDTH if h < SLICES - 1 else tail
            rows[k * SLICES + h : k * SLICES + h + 1, :width] = mine[:, h * WIDTH : h * WIDTH + width]
    out[...] = rows[...].astype(jnp.bfloat16).reshape(out.shape)


def weight_kernel(place, flux, ivar, mask, owner, keep, out, flux_in, ivar_in, mask_in, owner_in, sems):
    core = place[0]
    count, pixels = flux_in.shape
    height = 32
    copies = [(mask, mask_in), (owner, owner_in)]
    for at in range(0, count, height):
        copies += [(a.at[pl.ds(at, height), :], b.at[pl.ds(at, height), :]) for a, b in ((ivar, ivar_in), (flux, flux_in))]
    copies = [pltpu.make_async_copy(a, b, sems.at[i]) for i, (a, b) in enumerate(copies)]
    for copy in copies:
        copy.start()
    copies[0].wait()
    copies[1].wait()
    good = mask_in[...].astype(jnp.float32).T
    names = owner_in[...].astype(jnp.float32)
    out[count : count + 16, :] = jnp.zeros((16, pixels), jnp.bfloat16)
    out[count : count + 16, 0:count] = jnp.broadcast_to(names, (16, count)).astype(jnp.bfloat16)
    for i, at in enumerate(range(0, count, height)):
        copies[2 + 2 * i].wait()
        copies[3 + 2 * i].wait()
        for b in range(good.shape[1]):
            here = slice(at, at + height), slice(b * 128, (b + 1) * 128)
            flag = jnp.broadcast_to(good[at : at + height, b : b + 1], (height, 128)).astype(jnp.bfloat16)
            masked = (ivar_in[here] * flag).astype(jnp.float32)
            fluxes = masked * flux_in[here].astype(jnp.float32)
            keep[here] = jnp.where(core == 0, masked, fluxes).astype(jnp.bfloat16)
            out[here] = jnp.where(core == 0, fluxes, masked).astype(jnp.bfloat16)


def coadd_kernel(place, names, own, other, coadd):
    core = place[0]
    count, pixels = own.shape
    row = lax.broadcasted_iota(jnp.int32, (64, count), 0)
    wanted = jnp.where(row < 32, row + core * 32, row - core * 32).astype(jnp.float32)
    near = (names[...].astype(jnp.float32) == wanted).astype(jnp.float32)
    far = (other[count : count + 16, 0:count][0:1].astype(jnp.float32) == wanted).astype(jnp.float32)
    select = jnp.concatenate([near, far], axis=1).astype(jnp.bfloat16)
    for at in range(0, pixels, WIDTH):
        lanes = slice(at, min(at + WIDTH, pixels))
        spectra = jnp.concatenate([own[:, lanes], other[0:count, lanes]], axis=0)
        coadd[:, lanes] = jnp.dot(select, spectra, preferred_element_type=jnp.float32).astype(jnp.bfloat16)


def join_kernel(own, up, down, far, *halves):
    side = SLICES * 16
    row = lax.broadcasted_iota(jnp.int32, (side, side), 0)
    col = lax.broadcasted_iota(jnp.int32, (side, side), 1)
    same = ((row // 16) == (col % 16)) & ((row % 8) == (col // 32)) & ((row // 8) % 2 == (col // 16) % 2)
    order = same.astype(jnp.float32).astype(jnp.bfloat16)
    for m in range(HALVES):
        block = jnp.concatenate(
            [p[:, 2 * m : 2 * m + 2].reshape(p.shape[0] * 2 * SLICES, WIDTH) for p in (own, up, down, far)], axis=0
        )
        turned = jnp.dot(order, block, preferred_element_type=jnp.float32).astype(jnp.bfloat16)
        cut = halves[0].shape[0]
        for block in range(cut + halves[1].shape[0]):
            h, at = block // 4, block % 4 * 128
            out, place = (halves[0], block) if block < cut else (halves[1], block - cut)
            out[place, m] = turned[h * 16 : h * 16 + 16, at : at + 128]


def solve(entries, right):
    lower, scaled, inverse = {}, {}, []
    for j in range(TERMS):
        pivot = entries[j, j]
        for e in range(j):
            pivot = pivot - lower[j, e] * scaled[j, e]
        inverse.append(1.0 / pivot)
        for i in range(j + 1, TERMS):
            value = entries[j, i]
            for e in range(j):
                value = value - lower[i, e] * scaled[j, e]
            scaled[i, j] = value
            lower[i, j] = value * inverse[j]
    forward = []
    for i in range(TERMS):
        value = right[i]
        for e in range(i):
            value = value - lower[i, e] * forward[e]
        forward.append(value)
    answer = [None] * TERMS
    for i in reversed(range(TERMS)):
        value = forward[i] * inverse[i]
        for e in range(i + 1, TERMS):
            value = value - lower[e, i] * answer[e]
        answer[i] = value
    return answer


def fit_blocks(blocks, pixels, stacks, total):
    for at in range(0, pixels // 128, WIDTH // 128):
        taken = range(at, min(at + WIDTH // 128, pixels // 128))
        ivar, wflux = stacks(slice(at * 128, (at + len(taken)) * 128))
        for b, refs in enumerate(blocks):
            evens = []
            for m in range(HALVES):
                pieces = [refs[0][t, m] if t < refs[0].shape[0] else refs[1][t - refs[0].shape[0], m] for t in taken]
                evens.append(jnp.concatenate(pieces, axis=1))
            odds = [jnp.concatenate([e[8:16], e[0:8]], axis=0) for e in evens]
            products = jnp.concatenate(
                [evens[m] * (odds[n] if cross else evens[n]) for m, n, cross in combos()], axis=0
            )
            normal = jnp.dot(products, ivar, preferred_element_type=jnp.float32)
            project = jnp.dot(jnp.concatenate(evens, axis=0), wflux, preferred_element_type=jnp.float32)
            if at == 0:
                total[b, 0 : COMBOS * 16] = normal
                total[b, COMBOS * 16 : ROWS] = project
            else:
                total[b, 0 : COMBOS * 16] += normal
                total[b, COMBOS * 16 : ROWS] += project

    entries = {}
    for (k, l), at in entry_rows().items():
        value = total[:, at : at + 8, :]
        entries[k, l] = value + 1.0 if k == l else value
    right = [total[:, COMBOS * 16 + k * 8 : COMBOS * 16 + k * 8 + 8, :] for k in range(TERMS)]
    answer = solve(entries, right)
    gain = right[0] * answer[0]
    for k in range(1, TERMS):
        gain = gain + right[k] * answer[k]
    values = answer + [gain / TERMS, jnp.zeros_like(gain)]
    lane = lax.broadcasted_iota(jnp.int32, values[0].shape, 2) // 32
    packed = []
    for group in range(4):
        packed.append([])
        for q in range(3):
            out = None
            for k in range(4):
                shift = (k - group) % 4 * 32
                value = values[4 * q + k]
                value = pltpu.roll(value, shift, 2) if shift else value
                out = value if out is None else jnp.where(lane == k, value, out)
            packed[-1].append(out)
    return packed


def own_fit_kernel(place, own_a, own_b, mine, direct_a, direct_b, over, swapped_a, swapped_b, out, ivar, wflux, total):
    core = place[0]

    def stacks(span):
        near = jnp.concatenate([mine[:, span], direct_a[:, span], direct_b[:, span]], axis=0)
        far = jnp.concatenate([over[32:64, span], over[0:32, span], swapped_b[:, span], swapped_a[:, span]], axis=0)
        both = jnp.where(core == 0, near, far).T, jnp.where(core == 0, far, near).T
        ivar[span, :], wflux[span, :] = both
        return both

    packed = fit_blocks([[own_a, own_b]], mine.shape[1], stacks, total)
    for group in range(4):
        for q in range(3):
            out[group, :, q] = packed[group][q]


def near_fit_kernel(up_a, up_b, down_a, down_b, ivar, wflux, out, total):
    packed = fit_blocks([[up_a, up_b], [down_a, down_b]], ivar.shape[0], lambda span: (ivar[span, :], wflux[span, :]), total)
    for group in range(4):
        for q in range(3):
            out[group, :, q] = packed[group][q]


def far_fit_kernel(own, near, far_a, far_b, ivar, wflux, *rest):
    outs, total = rest[:4], rest[4]
    packed = fit_blocks([[far_a, far_b]], ivar.shape[0], lambda span: (ivar[span, :], wflux[span, :]), total)
    for group in range(4):
        outs[group][0:1] = own[group]
        outs[group][1:3] = near[group]
        for q in range(3):
            outs[group][3:4, q] = packed[group][q]


def final_kernel(place, counts, classes, part_0, part_1, part_2, part_3, coefs, gains, best):
    core, lo, hi, z, y = (place[i] for i in range(5))

    def shift(n):
        return jnp.where(n == 1, 3, jnp.where(n == 2, 1, jnp.where(n == 3, 2, 0)))

    def trial_of(i):
        group, b, t = i // 32, (i // 8) % 4, i % 8
        source_core = core ^ (group % 2)
        source_x = (2 * hi + lo + jnp.where(group < 2, 0, jnp.where(core == 0, 1, 3))) % 4
        near, far = shift(t // 2), shift(b)
        z_of = (z + jnp.where(source_core == 0, near, far)) % 4
        y_of = (y + jnp.where(source_core == 0, far, near)) % 4
        return (source_x // 2 ^ (t % 2)) * 64 + z_of * 16 + y_of * 4 + source_x % 2 * 2 + source_core

    trial = trial_of(lax.broadcasted_iota(jnp.int32, (128, 128), 0))
    lane = lax.broadcasted_iota(jnp.int32, (128, 128), 1)
    to_lane = (trial == lane).astype(jnp.float32).astype(jnp.bfloat16)
    end_0 = counts[0]
    end_1 = end_0 + counts[1]
    end_2 = end_1 + counts[2]
    trial_class = sum((trial >= end).astype(jnp.int32) for end in (end_0, end_1, end_2))
    stack = []
    for q in range(3):
        rows = jnp.concatenate([p[:, q].reshape(32, 128) for p in (part_0, part_1, part_2, part_3)], axis=0)
        if q == 2:
            drop = (lane // 32 == 2) & (trial_class != classes[...])
            rows = jnp.where(drop, 0.0, rows)
            best[...] = jnp.max(rows, axis=0, keepdims=True)[:, 64:96]
        rest = rows.T
        for _ in range(3):
            part = rest.astype(jnp.bfloat16)
            stack.append(part)
            rest = rest - part.astype(jnp.float32)
    turned = jnp.dot(jnp.concatenate(stack, axis=0), to_lane, preferred_element_type=jnp.float32)
    for k in range(TERMS + 1):
        at = k // 4 * 384 + k % 4 * 32
        value = turned[at : at + 32] + (turned[at + 128 : at + 160] + turned[at + 256 : at + 288])
        if k < TERMS:
            coefs[k] = value
        else:
            gains[...] = value


def cost(micros):
    return pl.CostEstimate(flops=int(micros * 1e9), bytes_accessed=int(micros * 3.0e6), transcendentals=0)


def body(flux, ivar, pixel_mask, exposure_target, basis, trial_counts, target_class):
    pixels = flux.shape[1]
    tmpl, spec, core = (lax.axis_index(a) for a in AXES)
    place = jnp.stack([core, spec % 2, tmpl // 4, tmpl % 4, spec // 2]).astype(jnp.int32)
    smem = pl.BlockSpec(memory_space=pltpu.SMEM)
    vmem = pl.BlockSpec(memory_space=pltpu.VMEM)
    params = pltpu.CompilerParams(vmem_limit_bytes=VMEM)

    trial = pl.pallas_call(
        prep_kernel,
        out_shape=jax.ShapeDtypeStruct((1, TERMS, SLICES, WIDTH), jnp.bfloat16),
        in_specs=[smem, vmem],
        out_specs=vmem,
        scratch_shapes=[pltpu.VMEM((TERMS * SLICES, WIDTH), jnp.float32)],
        compiler_params=params,
        cost_estimate=cost(0.7),
        name="prep",
    )(place, jnp.transpose(basis, (1, 0, 2)))
    other = send(trial, x_hi=1)
    pair = jnp.concatenate([trial, other], axis=0)

    count = flux.shape[0]
    owners = exposure_target.reshape(1, count)
    views = (flux, ivar, pixel_mask.T, owners)
    keep, outgoing = pl.pallas_call(
        weight_kernel,
        out_shape=(
            jax.ShapeDtypeStruct((count, pixels), jnp.bfloat16),
            jax.ShapeDtypeStruct((count + 16, pixels), jnp.bfloat16),
        ),
        in_specs=[smem] + [pl.BlockSpec(memory_space=pltpu.HBM)] * 4,
        out_specs=(vmem,) * 2,
        scratch_shapes=[pltpu.VMEM(v.shape, v.dtype) for v in views] + [pltpu.SemaphoreType.DMA((8,))],
        compiler_params=params,
        cost_estimate=cost(2.3),
        name="weight",
    )(place, *(pltpu.with_memory_space_constraint(v, pltpu.HBM) for v in views))
    outgoing, _ = lax.optimization_barrier((outgoing, other))
    incoming = send(outgoing, core=1)

    mine = pl.pallas_call(
        coadd_kernel,
        out_shape=jax.ShapeDtypeStruct((64, pixels), jnp.bfloat16),
        in_specs=[smem] + [vmem] * 3,
        out_specs=vmem,
        compiler_params=params,
        cost_estimate=cost(2.4),
        name="coadd",
    )(place, owners, keep, incoming)
    direct = send(mine[:32], x=1), send(mine[32:], x=-1)
    late, _ = lax.optimization_barrier((mine, direct[0]))
    over = send(late, core=1)
    swapped = [send(v, core=1) for v in direct]

    near = [pair] + [send(pair, along=0, step=s) for s in (1, -1, 2)]

    near[0], mine = lax.optimization_barrier((near[0], mine))
    cut = pixels // 256
    eight = pl.pallas_call(
        join_kernel,
        out_shape=tuple(jax.ShapeDtypeStruct((n, HALVES, 16, 128), jnp.bfloat16) for n in (cut, pixels // 128 - cut)),
        in_specs=[vmem] * 4,
        out_specs=(vmem,) * 2,
        compiler_params=params,
        cost_estimate=cost(0.5),
        name="join",
    )(*near)
    up_a, down_b = send(eight[0], along=1, step=1), send(eight[1], along=1, step=-1)
    up_b, down_a = send(eight[1], along=1, step=1), send(eight[0], along=1, step=-1)
    far = send(up_a, along=1, step=1), send(down_b, along=1, step=-1)

    def fit(kernel, operands, shapes, count, micros, name):
        return pl.pallas_call(
            kernel,
            out_shape=shapes,
            in_specs=[smem if v is place else vmem for v in operands],
            out_specs=(vmem,) * len(shapes),
            scratch_shapes=[pltpu.VMEM((count, ROWS, 128), jnp.float32)],
            compiler_params=params,
            cost_estimate=cost(micros),
            name=name,
        )(*operands)

    stack = jax.ShapeDtypeStruct((pixels, 128), jnp.bfloat16)

    def packed(*sizes):
        return jax.ShapeDtypeStruct(sizes + (3, 8, 128), jnp.float32)

    own, *stacks = fit(
        own_fit_kernel, (place, *eight, mine, *direct, over, *swapped), (packed(4, 1), stack, stack), 1, 0, "own_fit"
    )
    (near,) = fit(near_fit_kernel, (up_a, up_b, down_a, down_b, *stacks), (packed(4, 2),), 2, 6, "near_fit")
    parts = fit(far_fit_kernel, (own, near, *far, *stacks), (packed(4),) * 4, 1, 3, "far_fit")

    parts = (
        parts[0],
        send(parts[1], core=1),
        send(parts[2], x=-1),
        send(parts[3], x=1, core=1),
    )
    coefs, gains, best = pl.pallas_call(
        final_kernel,
        out_shape=(
            jax.ShapeDtypeStruct((TERMS, 32, 128), jnp.float32),
            jax.ShapeDtypeStruct((32, 128), jnp.float32),
            jax.ShapeDtypeStruct((1, 32), jnp.float32),
        ),
        in_specs=[smem, smem] + [vmem] * 5,
        out_specs=(vmem,) * 3,
        compiler_params=params,
        cost_estimate=cost(2),
        name="final",
    )(place, trial_counts, jnp.tile(target_class, 4).reshape(1, 128), *parts)
    return coefs, gains, best.reshape(32)


def solution(mesh):
    rows = P(AXES, None)
    return jax.shard_map(
        body,
        mesh=mesh,
        in_specs=(rows, rows, rows, P(AXES), P(("tmpl", "spec"), None, None), P(), P(AXES)),
        out_specs=(P(None, AXES, None), P(AXES, None), P(AXES)),
        check_vma=False,
    )
```

```python
import jax
import jax.numpy as jnp
import numpy as np
from jax import lax
from jax.experimental import pallas as pl
from jax.experimental.pallas import tpu as pltpu
from jax.sharding import PartitionSpec as P

AXES = ("tmpl", "spec", "expo")
SIDES = (2, 4, 4, 2, 2)
TERMS = 10
HALVES = TERMS // 2
SLICES = 16
WIDTH = 512
COMBOS = 30
ROWS = COMBOS * 16 + TERMS * 8
VMEM = 24 * 1024 * 1024


def moved(device, core=0, x_hi=0, x=0, along=None, step=0):
    h, z, y, lo, c = (int(v) for v in np.unravel_index(device, SIDES))
    if along is not None:
        if (c == 0) == (along == 0):
            z = (z + step) % 4
        else:
            y = (y + step) % 4
    h, lo = divmod((2 * h + lo + (x if c == 0 else -x)) % 4, 2)
    return int(np.ravel_multi_index((h ^ x_hi, z, y, lo, c ^ core), SIDES))


def send(value, **how):
    return lax.ppermute(value, AXES, [(d, moved(d, **how)) for d in range(128)])


def combos():
    out = [(m, n, 0) for m in range(HALVES) for n in range(m + 1, HALVES)]
    out += [(m, n, 1) for m in range(HALVES) for n in range(m + 1, HALVES)]
    out += [(m, m, 0) for m in range(HALVES)]
    out += [(m, m, 1) for m in range(HALVES)]
    return out


def entry_rows():
    where = {}
    for i, (m, n, crossed) in enumerate(combos()):
        for half in range(2):
            k, l = 2 * m + half, 2 * n + (half ^ crossed)
            where.setdefault((min(k, l), max(k, l)), i * 16 + half * 8)
    return where


def prep_kernel(place, basis, out, rows):
    core = place[0]
    pixels = basis.shape[2]
    tail = pixels - (SLICES - 1) * WIDTH
    rows[...] = jnp.zeros_like(rows)
    for k in range(TERMS):
        both = basis[k].astype(jnp.float32)
        mine = jnp.where(core == 0, both[0:1], both[1:2])
        for h in range(SLICES):
            width = WIDTH if h < SLICES - 1 else tail
            rows[k * SLICES + h : k * SLICES + h + 1, :width] = mine[:, h * WIDTH : h * WIDTH + width]
    out[...] = rows[...].astype(jnp.bfloat16).reshape(out.shape)


def weight_kernel(place, flux, ivar, mask, owner, keep, out, flux_in, ivar_in, mask_in, owner_in, sems):
    core = place[0]
    count, pixels = flux_in.shape
    height = 32
    copies = [(mask, mask_in), (owner, owner_in)]
    for at in range(0, count, height):
        copies += [(a.at[pl.ds(at, height), :], b.at[pl.ds(at, height), :]) for a, b in ((ivar, ivar_in), (flux, flux_in))]
    copies = [pltpu.make_async_copy(a, b, sems.at[i]) for i, (a, b) in enumerate(copies)]
    for copy in copies:
        copy.start()
    copies[0].wait()
    copies[1].wait()
    good = mask_in[...].astype(jnp.float32).T
    names = owner_in[...].astype(jnp.float32)
    out[count : count + 16, :] = jnp.zeros((16, pixels), jnp.bfloat16)
    out[count : count + 16, 0:count] = jnp.broadcast_to(names, (16, count)).astype(jnp.bfloat16)
    for i, at in enumerate(range(0, count, height)):
        copies[2 + 2 * i].wait()
        copies[3 + 2 * i].wait()
        for b in range(good.shape[1]):
            here = slice(at, at + height), slice(b * 128, (b + 1) * 128)
            flag = jnp.broadcast_to(good[at : at + height, b : b + 1], (height, 128)).astype(jnp.bfloat16)
            masked = (ivar_in[here] * flag).astype(jnp.float32)
            fluxes = masked * flux_in[here].astype(jnp.float32)
            keep[here] = jnp.where(core == 0, masked, fluxes).astype(jnp.bfloat16)
            out[here] = jnp.where(core == 0, fluxes, masked).astype(jnp.bfloat16)


def coadd_kernel(place, names, own, other, coadd):
    core = place[0]
    count, pixels = own.shape
    row = lax.broadcasted_iota(jnp.int32, (64, count), 0)
    wanted = jnp.where(row < 32, row + core * 32, row - core * 32).astype(jnp.float32)
    near = (names[...].astype(jnp.float32) == wanted).astype(jnp.float32)
    far = (other[count : count + 16, 0:count][0:1].astype(jnp.float32) == wanted).astype(jnp.float32)
    select = jnp.concatenate([near, far], axis=1).astype(jnp.bfloat16)
    for at in range(0, pixels, WIDTH):
        lanes = slice(at, min(at + WIDTH, pixels))
        spectra = jnp.concatenate([own[:, lanes], other[0:count, lanes]], axis=0)
        coadd[:, lanes] = jnp.dot(select, spectra, preferred_element_type=jnp.float32).astype(jnp.bfloat16)


def join_kernel(own, up, down, far, *halves):
    side = SLICES * 16
    row = lax.broadcasted_iota(jnp.int32, (side, side), 0)
    col = lax.broadcasted_iota(jnp.int32, (side, side), 1)
    same = ((row // 16) == (col % 16)) & ((row % 8) == (col // 32)) & ((row // 8) % 2 == (col // 16) % 2)
    order = same.astype(jnp.float32).astype(jnp.bfloat16)
    for m in range(HALVES):
        block = jnp.concatenate(
            [p[:, 2 * m : 2 * m + 2].reshape(p.shape[0] * 2 * SLICES, WIDTH) for p in (own, up, down, far)], axis=0
        )
        turned = jnp.dot(order, block, preferred_element_type=jnp.float32).astype(jnp.bfloat16)
        cut = halves[0].shape[0]
        for block in range(cut + halves[1].shape[0]):
            h, at = block // 4, block % 4 * 128
            out, place = (halves[0], block) if block < cut else (halves[1], block - cut)
            out[place, m] = turned[h * 16 : h * 16 + 16, at : at + 128]


def solve(entries, right):
    lower, scaled, inverse = {}, {}, []
    for j in range(TERMS):
        pivot = entries[j, j]
        for e in range(j):
            pivot = pivot - lower[j, e] * scaled[j, e]
        inverse.append(1.0 / pivot)
        for i in range(j + 1, TERMS):
            value = entries[j, i]
            for e in range(j):
                value = value - lower[i, e] * scaled[j, e]
            scaled[i, j] = value
            lower[i, j] = value * inverse[j]
    forward = []
    for i in range(TERMS):
        value = right[i]
        for e in range(i):
            value = value - lower[i, e] * forward[e]
        forward.append(value)
    answer = [None] * TERMS
    for i in reversed(range(TERMS)):
        value = forward[i] * inverse[i]
        for e in range(i + 1, TERMS):
            value = value - lower[e, i] * answer[e]
        answer[i] = value
    return answer


def fit_blocks(blocks, pixels, stacks, total):
    for at in range(0, pixels // 128, WIDTH // 128):
        taken = range(at, min(at + WIDTH // 128, pixels // 128))
        ivar, wflux = stacks(slice(at * 128, (at + len(taken)) * 128))
        for b, refs in enumerate(blocks):
            evens = []
            for m in range(HALVES):
                pieces = [refs[0][t, m] if t < refs[0].shape[0] else refs[1][t - refs[0].shape[0], m] for t in taken]
                evens.append(jnp.concatenate(pieces, axis=1))
            odds = [jnp.concatenate([e[8:16], e[0:8]], axis=0) for e in evens]
            products = jnp.concatenate(
                [evens[m] * (odds[n] if cross else evens[n]) for m, n, cross in combos()], axis=0
            )
            normal = jnp.dot(products, ivar, preferred_element_type=jnp.float32)
            project = jnp.dot(jnp.concatenate(evens, axis=0), wflux, preferred_element_type=jnp.float32)
            if at == 0:
                total[b, 0 : COMBOS * 16] = normal
                total[b, COMBOS * 16 : ROWS] = project
            else:
                total[b, 0 : COMBOS * 16] += normal
                total[b, COMBOS * 16 : ROWS] += project

    entries = {}
    for (k, l), at in entry_rows().items():
        value = total[:, at : at + 8, :]
        entries[k, l] = value + 1.0 if k == l else value
    right = [total[:, COMBOS * 16 + k * 8 : COMBOS * 16 + k * 8 + 8, :] for k in range(TERMS)]
    answer = solve(entries, right)
    gain = right[0] * answer[0]
    for k in range(1, TERMS):
        gain = gain + right[k] * answer[k]
    values = answer + [gain / TERMS, jnp.zeros_like(gain)]
    lane = lax.broadcasted_iota(jnp.int32, values[0].shape, 2) // 32
    packed = []
    for group in range(4):
        packed.append([])
        for q in range(3):
            out = None
            for k in range(4):
                shift = (k - group) % 4 * 32
                value = values[4 * q + k]
                value = pltpu.roll(value, shift, 2) if shift else value
                out = value if out is None else jnp.where(lane == k, value, out)
            packed[-1].append(out)
    return packed


def own_fit_kernel(place, own_a, own_b, mine, direct_a, direct_b, over, swapped_a, swapped_b, out, ivar, wflux, total):
    core = place[0]

    def stacks(span):
        near = jnp.concatenate([mine[:, span], direct_a[:, span], direct_b[:, span]], axis=0)
        far = jnp.concatenate([over[32:64, span], over[0:32, span], swapped_b[:, span], swapped_a[:, span]], axis=0)
        both = jnp.where(core == 0, near, far).T, jnp.where(core == 0, far, near).T
        ivar[span, :], wflux[span, :] = both
        return both

    packed = fit_blocks([[own_a, own_b]], mine.shape[1], stacks, total)
    for group in range(4):
        for q in range(3):
            out[group, :, q] = packed[group][q]


def near_fit_kernel(up_a, up_b, down_a, down_b, ivar, wflux, out, total):
    packed = fit_blocks([[up_a, up_b], [down_a, down_b]], ivar.shape[0], lambda span: (ivar[span, :], wflux[span, :]), total)
    for group in range(4):
        for q in range(3):
            out[group, :, q] = packed[group][q]


def far_fit_kernel(own, near, far_a, far_b, ivar, wflux, *rest):
    outs, total = rest[:4], rest[4]
    packed = fit_blocks([[far_a, far_b]], ivar.shape[0], lambda span: (ivar[span, :], wflux[span, :]), total)
    for group in range(4):
        outs[group][0:1] = own[group]
        outs[group][1:3] = near[group]
        for q in range(3):
            outs[group][3:4, q] = packed[group][q]


def final_kernel(place, counts, classes, part_0, part_1, part_2, part_3, coefs, gains, best):
    core, lo, hi, z, y = (place[i] for i in range(5))

    def shift(n):
        return jnp.where(n == 1, 3, jnp.where(n == 2, 1, jnp.where(n == 3, 2, 0)))

    def trial_of(i):
        group, b, t = i // 32, (i // 8) % 4, i % 8
        source_core = core ^ (group % 2)
        source_x = (2 * hi + lo + jnp.where(group < 2, 0, jnp.where(core == 0, 1, 3))) % 4
        near, far = shift(t // 2), shift(b)
        z_of = (z + jnp.where(source_core == 0, near, far)) % 4
        y_of = (y + jnp.where(source_core == 0, far, near)) % 4
        return (source_x // 2 ^ (t % 2)) * 64 + z_of * 16 + y_of * 4 + source_x % 2 * 2 + source_core

    trial = trial_of(lax.broadcasted_iota(jnp.int32, (128, 128), 0))
    lane = lax.broadcasted_iota(jnp.int32, (128, 128), 1)
    to_lane = (trial == lane).astype(jnp.float32).astype(jnp.bfloat16)
    end_0 = counts[0]
    end_1 = end_0 + counts[1]
    end_2 = end_1 + counts[2]
    trial_class = sum((trial >= end).astype(jnp.int32) for end in (end_0, end_1, end_2))
    stack = []
    for q in range(3):
        rows = jnp.concatenate([p[:, q].reshape(32, 128) for p in (part_0, part_1, part_2, part_3)], axis=0)
        if q == 2:
            drop = (lane // 32 == 2) & (trial_class != classes[...])
            rows = jnp.where(drop, 0.0, rows)
            best[...] = jnp.max(rows, axis=0, keepdims=True)[:, 64:96]
        rest = rows.T
        for _ in range(3):
            part = rest.astype(jnp.bfloat16)
            stack.append(part)
            rest = rest - part.astype(jnp.float32)
    turned = jnp.dot(jnp.concatenate(stack, axis=0), to_lane, preferred_element_type=jnp.float32)
    for k in range(TERMS + 1):
        at = k // 4 * 384 + k % 4 * 32
        value = turned[at : at + 32] + (turned[at + 128 : at + 160] + turned[at + 256 : at + 288])
        if k < TERMS:
            coefs[k] = value
        else:
            gains[...] = value


def cost(micros):
    return pl.CostEstimate(flops=int(micros * 1e9), bytes_accessed=int(micros * 3.0e6), transcendentals=0)


def body(flux, ivar, pixel_mask, exposure_target, basis, trial_counts, target_class):
    pixels = flux.shape[1]
    tmpl, spec, core = (lax.axis_index(a) for a in AXES)
    place = jnp.stack([core, spec % 2, tmpl // 4, tmpl % 4, spec // 2]).astype(jnp.int32)
    smem = pl.BlockSpec(memory_space=pltpu.SMEM)
    vmem = pl.BlockSpec(memory_space=pltpu.VMEM)
    params = pltpu.CompilerParams(vmem_limit_bytes=VMEM)

    trial = pl.pallas_call(
        prep_kernel,
        out_shape=jax.ShapeDtypeStruct((1, TERMS, SLICES, WIDTH), jnp.bfloat16),
        in_specs=[smem, vmem],
        out_specs=vmem,
        scratch_shapes=[pltpu.VMEM((TERMS * SLICES, WIDTH), jnp.float32)],
        compiler_params=params,
        cost_estimate=cost(0.7),
        name="prep",
    )(place, jnp.transpose(basis, (1, 0, 2)))
    other = send(trial, x_hi=1)
    pair = jnp.concatenate([trial, other], axis=0)

    count = flux.shape[0]
    owners = exposure_target.reshape(1, count)
    views = (flux, ivar, pixel_mask.T, owners)
    keep, outgoing = pl.pallas_call(
        weight_kernel,
        out_shape=(
            jax.ShapeDtypeStruct((count, pixels), jnp.bfloat16),
            jax.ShapeDtypeStruct((count + 16, pixels), jnp.bfloat16),
        ),
        in_specs=[smem] + [pl.BlockSpec(memory_space=pltpu.HBM)] * 4,
        out_specs=(vmem,) * 2,
        scratch_shapes=[pltpu.VMEM(v.shape, v.dtype) for v in views] + [pltpu.SemaphoreType.DMA((8,))],
        compiler_params=params,
        cost_estimate=cost(2.3),
        name="weight",
    )(place, *(pltpu.with_memory_space_constraint(v, pltpu.HBM) for v in views))
    outgoing, _ = lax.optimization_barrier((outgoing, other))
    incoming = send(outgoing, core=1)

    mine = pl.pallas_call(
        coadd_kernel,
        out_shape=jax.ShapeDtypeStruct((64, pixels), jnp.bfloat16),
        in_specs=[smem] + [vmem] * 3,
        out_specs=vmem,
        compiler_params=params,
        cost_estimate=cost(2.4),
        name="coadd",
    )(place, owners, keep, incoming)
    direct = send(mine[:32], x=1), send(mine[32:], x=-1)
    late, _ = lax.optimization_barrier((mine, direct))
    over = send(late, core=1)
    swapped = [send(v, core=1) for v in direct]

    near = [pair] + [send(pair, along=0, step=s) for s in (1, -1, 2)]

    near[0], mine = lax.optimization_barrier((near[0], mine))
    cut = pixels // 256
    eight = pl.pallas_call(
        join_kernel,
        out_shape=tuple(jax.ShapeDtypeStruct((n, HALVES, 16, 128), jnp.bfloat16) for n in (cut, pixels // 128 - cut)),
        in_specs=[vmem] * 4,
        out_specs=(vmem,) * 2,
        compiler_params=params,
        cost_estimate=cost(0.5),
        name="join",
    )(*near)
    up_a, down_b = send(eight[0], along=1, step=1), send(eight[1], along=1, step=-1)
    up_b, down_a = send(eight[1], along=1, step=1), send(eight[0], along=1, step=-1)
    far = send(up_a, along=1, step=1), send(down_b, along=1, step=-1)

    def fit(kernel, operands, shapes, count, micros, name):
        return pl.pallas_call(
            kernel,
            out_shape=shapes,
            in_specs=[smem if v is place else vmem for v in operands],
            out_specs=(vmem,) * len(shapes),
            scratch_shapes=[pltpu.VMEM((count, ROWS, 128), jnp.float32)],
            compiler_params=params,
            cost_estimate=cost(micros),
            name=name,
        )(*operands)

    stack = jax.ShapeDtypeStruct((pixels, 128), jnp.bfloat16)

    def packed(*sizes):
        return jax.ShapeDtypeStruct(sizes + (3, 8, 128), jnp.float32)

    own, *stacks = fit(
        own_fit_kernel, (place, *eight, mine, *direct, over, *swapped), (packed(4, 1), stack, stack), 1, 0, "own_fit"
    )
    (near,) = fit(near_fit_kernel, (up_a, up_b, down_a, down_b, *stacks), (packed(4, 2),), 2, 6, "near_fit")
    parts = fit(far_fit_kernel, (own, near, *far, *stacks), (packed(4),) * 4, 1, 3, "far_fit")

    parts = (
        parts[0],
        send(parts[1], core=1),
        send(parts[2], x=-1),
        send(parts[3], x=1, core=1),
    )
    coefs, gains, best = pl.pallas_call(
        final_kernel,
        out_shape=(
            jax.ShapeDtypeStruct((TERMS, 32, 128), jnp.float32),
            jax.ShapeDtypeStruct((32, 128), jnp.float32),
            jax.ShapeDtypeStruct((1, 32), jnp.float32),
        ),
        in_specs=[smem, smem] + [vmem] * 5,
        out_specs=(vmem,) * 3,
        compiler_params=params,
        cost_estimate=cost(2),
        name="final",
    )(place, trial_counts, jnp.tile(target_class, 4).reshape(1, 128), *parts)
    return coefs, gains, best.reshape(32)


def solution(mesh):
    rows = P(AXES, None)
    return jax.shard_map(
        body,
        mesh=mesh,
        in_specs=(rows, rows, rows, P(AXES), P(("tmpl", "spec"), None, None), P(), P(AXES)),
        out_specs=(P(None, AXES, None), P(AXES, None), P(AXES)),
        check_vma=False,
    )
```

```python
import jax
import jax.numpy as jnp
import numpy as np
from jax import lax
from jax.experimental import pallas as pl
from jax.experimental.pallas import tpu as pltpu
from jax.sharding import PartitionSpec as P

AXES = ("tmpl", "spec", "expo")
SIDES = (2, 4, 4, 2, 2)
TERMS = 10
HALVES = TERMS // 2
SLICES = 16
WIDTH = 512
COMBOS = 30
ROWS = COMBOS * 16 + TERMS * 8
VMEM = 24 * 1024 * 1024


def moved(device, core=0, x_hi=0, x=0, along=None, step=0):
    h, z, y, lo, c = (int(v) for v in np.unravel_index(device, SIDES))
    if along is not None:
        if (c == 0) == (along == 0):
            z = (z + step) % 4
        else:
            y = (y + step) % 4
    h, lo = divmod((2 * h + lo + (x if c == 0 else -x)) % 4, 2)
    return int(np.ravel_multi_index((h ^ x_hi, z, y, lo, c ^ core), SIDES))


def send(value, **how):
    return lax.ppermute(value, AXES, [(d, moved(d, **how)) for d in range(128)])


def combos():
    out = [(m, n, 0) for m in range(HALVES) for n in range(m + 1, HALVES)]
    out += [(m, n, 1) for m in range(HALVES) for n in range(m + 1, HALVES)]
    out += [(m, m, 0) for m in range(HALVES)]
    out += [(m, m, 1) for m in range(HALVES)]
    return out


def entry_rows():
    where = {}
    for i, (m, n, crossed) in enumerate(combos()):
        for half in range(2):
            k, l = 2 * m + half, 2 * n + (half ^ crossed)
            where.setdefault((min(k, l), max(k, l)), i * 16 + half * 8)
    return where


def prep_kernel(place, basis, out, rows):
    core = place[0]
    pixels = basis.shape[2]
    tail = pixels - (SLICES - 1) * WIDTH
    rows[...] = jnp.zeros_like(rows)
    for k in range(TERMS):
        both = basis[k].astype(jnp.float32)
        mine = jnp.where(core == 0, both[0:1], both[1:2])
        for h in range(SLICES):
            width = WIDTH if h < SLICES - 1 else tail
            rows[k * SLICES + h : k * SLICES + h + 1, :width] = mine[:, h * WIDTH : h * WIDTH + width]
    out[...] = rows[...].astype(jnp.bfloat16).reshape(out.shape)


def weight_kernel(place, flux, ivar, mask, owner, keep, out, flux_in, ivar_in, mask_in, owner_in, sems):
    core = place[0]
    count, pixels = flux_in.shape
    height = 32
    copies = [(mask, mask_in), (owner, owner_in)]
    for at in range(0, count, height):
        copies += [(a.at[pl.ds(at, height), :], b.at[pl.ds(at, height), :]) for a, b in ((ivar, ivar_in), (flux, flux_in))]
    copies = [pltpu.make_async_copy(a, b, sems.at[i]) for i, (a, b) in enumerate(copies)]
    for copy in copies:
        copy.start()
    copies[0].wait()
    copies[1].wait()
    good = mask_in[...].astype(jnp.float32).T
    names = owner_in[...].astype(jnp.float32)
    out[count : count + 16, :] = jnp.zeros((16, pixels), jnp.bfloat16)
    out[count : count + 16, 0:count] = jnp.broadcast_to(names, (16, count)).astype(jnp.bfloat16)
    for i, at in enumerate(range(0, count, height)):
        copies[2 + 2 * i].wait()
        copies[3 + 2 * i].wait()
        for b in range(good.shape[1]):
            here = slice(at, at + height), slice(b * 128, (b + 1) * 128)
            flag = jnp.broadcast_to(good[at : at + height, b : b + 1], (height, 128)).astype(jnp.bfloat16)
            masked = (ivar_in[here] * flag).astype(jnp.float32)
            fluxes = masked * flux_in[here].astype(jnp.float32)
            keep[here] = jnp.where(core == 0, masked, fluxes).astype(jnp.bfloat16)
            out[here] = jnp.where(core == 0, fluxes, masked).astype(jnp.bfloat16)


def coadd_kernel(place, names, own, other, coadd):
    core = place[0]
    count, pixels = own.shape
    row = lax.broadcasted_iota(jnp.int32, (64, count), 0)
    wanted = jnp.where(row < 32, row + core * 32, row - core * 32).astype(jnp.float32)
    near = (names[...].astype(jnp.float32) == wanted).astype(jnp.float32)
    far = (other[count : count + 16, 0:count][0:1].astype(jnp.float32) == wanted).astype(jnp.float32)
    select = jnp.concatenate([near, far], axis=1).astype(jnp.bfloat16)
    for at in range(0, pixels, WIDTH):
        lanes = slice(at, min(at + WIDTH, pixels))
        spectra = jnp.concatenate([own[:, lanes], other[0:count, lanes]], axis=0)
        coadd[:, lanes] = jnp.dot(select, spectra, preferred_element_type=jnp.float32).astype(jnp.bfloat16)


def join_kernel(own, up, down, far, *halves):
    side = SLICES * 16
    row = lax.broadcasted_iota(jnp.int32, (side, side), 0)
    col = lax.broadcasted_iota(jnp.int32, (side, side), 1)
    same = ((row // 16) == (col % 16)) & ((row % 8) == (col // 32)) & ((row // 8) % 2 == (col // 16) % 2)
    order = same.astype(jnp.float32).astype(jnp.bfloat16)
    for m in range(HALVES):
        block = jnp.concatenate(
            [p[:, 2 * m : 2 * m + 2].reshape(p.shape[0] * 2 * SLICES, WIDTH) for p in (own, up, down, far)], axis=0
        )
        turned = jnp.dot(order, block, preferred_element_type=jnp.float32).astype(jnp.bfloat16)
        cut = halves[0].shape[0]
        for block in range(cut + halves[1].shape[0]):
            h, at = block // 4, block % 4 * 128
            out, place = (halves[0], block) if block < cut else (halves[1], block - cut)
            out[place, m] = turned[h * 16 : h * 16 + 16, at : at + 128]


def solve(entries, right):
    lower, scaled, inverse = {}, {}, []
    for j in range(TERMS):
        pivot = entries[j, j]
        for e in range(j):
            pivot = pivot - lower[j, e] * scaled[j, e]
        inverse.append(1.0 / pivot)
        for i in range(j + 1, TERMS):
            value = entries[j, i]
            for e in range(j):
                value = value - lower[i, e] * scaled[j, e]
            scaled[i, j] = value
            lower[i, j] = value * inverse[j]
    forward = []
    for i in range(TERMS):
        value = right[i]
        for e in range(i):
            value = value - lower[i, e] * forward[e]
        forward.append(value)
    answer = [None] * TERMS
    for i in reversed(range(TERMS)):
        value = forward[i] * inverse[i]
        for e in range(i + 1, TERMS):
            value = value - lower[e, i] * answer[e]
        answer[i] = value
    return answer


def fit_blocks(blocks, pixels, stacks, total):
    for at in range(0, pixels // 128, WIDTH // 128):
        taken = range(at, min(at + WIDTH // 128, pixels // 128))
        ivar, wflux = stacks(slice(at * 128, (at + len(taken)) * 128))
        for b, refs in enumerate(blocks):
            evens = []
            for m in range(HALVES):
                pieces = [refs[0][t, m] if t < refs[0].shape[0] else refs[1][t - refs[0].shape[0], m] for t in taken]
                evens.append(jnp.concatenate(pieces, axis=1))
            odds = [jnp.concatenate([e[8:16], e[0:8]], axis=0) for e in evens]
            products = jnp.concatenate(
                [evens[m] * (odds[n] if cross else evens[n]) for m, n, cross in combos()], axis=0
            )
            normal = jnp.dot(products, ivar, preferred_element_type=jnp.float32)
            project = jnp.dot(jnp.concatenate(evens, axis=0), wflux, preferred_element_type=jnp.float32)
            if at == 0:
                total[b, 0 : COMBOS * 16] = normal
                total[b, COMBOS * 16 : ROWS] = project
            else:
                total[b, 0 : COMBOS * 16] += normal
                total[b, COMBOS * 16 : ROWS] += project

    entries = {}
    for (k, l), at in entry_rows().items():
        value = total[:, at : at + 8, :]
        entries[k, l] = value + 1.0 if k == l else value
    right = [total[:, COMBOS * 16 + k * 8 : COMBOS * 16 + k * 8 + 8, :] for k in range(TERMS)]
    answer = solve(entries, right)
    gain = right[0] * answer[0]
    for k in range(1, TERMS):
        gain = gain + right[k] * answer[k]
    values = answer + [gain / TERMS, jnp.zeros_like(gain)]
    lane = lax.broadcasted_iota(jnp.int32, values[0].shape, 2) // 32
    packed = []
    for group in range(4):
        packed.append([])
        for q in range(3):
            out = None
            for k in range(4):
                shift = (k - group) % 4 * 32
                value = values[4 * q + k]
                value = pltpu.roll(value, shift, 2) if shift else value
                out = value if out is None else jnp.where(lane == k, value, out)
            packed[-1].append(out)
    return packed


def own_fit_kernel(place, own_a, own_b, mine, direct_a, direct_b, over, swapped_a, swapped_b, out, ivar, wflux, total):
    core = place[0]

    def stacks(span):
        near = jnp.concatenate([mine[:, span], direct_a[:, span], direct_b[:, span]], axis=0)
        far = jnp.concatenate([over[32:64, span], over[0:32, span], swapped_b[:, span], swapped_a[:, span]], axis=0)
        both = jnp.where(core == 0, near, far).T, jnp.where(core == 0, far, near).T
        ivar[span, :], wflux[span, :] = both
        return both

    packed = fit_blocks([[own_a, own_b]], mine.shape[1], stacks, total)
    for group in range(4):
        for q in range(3):
            out[group, :, q] = packed[group][q]


def near_fit_kernel(up_a, up_b, down_a, down_b, ivar, wflux, out, total):
    packed = fit_blocks([[up_a, up_b], [down_a, down_b]], ivar.shape[0], lambda span: (ivar[span, :], wflux[span, :]), total)
    for group in range(4):
        for q in range(3):
            out[group, :, q] = packed[group][q]


def far_fit_kernel(own, near, far_a, far_b, ivar, wflux, *rest):
    outs, total = rest[:4], rest[4]
    packed = fit_blocks([[far_a, far_b]], ivar.shape[0], lambda span: (ivar[span, :], wflux[span, :]), total)
    for group in range(4):
        outs[group][0:1] = own[group]
        outs[group][1:3] = near[group]
        for q in range(3):
            outs[group][3:4, q] = packed[group][q]


def trial_order(place, counts, classes, to_lane, drop):
    core, lo, hi, z, y = (place[i] for i in range(5))

    def shift(n):
        return jnp.where(n == 1, 3, jnp.where(n == 2, 1, jnp.where(n == 3, 2, 0)))

    def trial_of(i):
        group, b, t = i // 32, (i // 8) % 4, i % 8
        source_core = core ^ (group % 2)
        source_x = (2 * hi + lo + jnp.where(group < 2, 0, jnp.where(core == 0, 1, 3))) % 4
        near, far = shift(t // 2), shift(b)
        z_of = (z + jnp.where(source_core == 0, near, far)) % 4
        y_of = (y + jnp.where(source_core == 0, far, near)) % 4
        return (source_x // 2 ^ (t % 2)) * 64 + z_of * 16 + y_of * 4 + source_x % 2 * 2 + source_core

    trial = trial_of(lax.broadcasted_iota(jnp.int32, (128, 128), 0))
    lane = lax.broadcasted_iota(jnp.int32, (128, 128), 1)
    to_lane[...] = (trial == lane).astype(jnp.float32).astype(jnp.bfloat16)
    end_0 = counts[0]
    end_1 = end_0 + counts[1]
    end_2 = end_1 + counts[2]
    trial_class = sum((trial >= end).astype(jnp.int32) for end in (end_0, end_1, end_2))
    drop[...] = ((lane // 32 == 2) & (trial_class != classes[...])).astype(jnp.float32)


def final_kernel(to_lane, drop, part_0, part_1, part_2, part_3, coefs, gains, best):
    stack = []
    for q in range(3):
        rows = jnp.concatenate([p[:, q].reshape(32, 128) for p in (part_0, part_1, part_2, part_3)], axis=0)
        if q == 2:
            rows = jnp.where(drop[...] > 0.0, 0.0, rows)
            best[...] = jnp.max(rows, axis=0, keepdims=True)[:, 64:96]
        rest = rows.T
        for _ in range(3):
            part = rest.astype(jnp.bfloat16)
            stack.append(part)
            rest = rest - part.astype(jnp.float32)
    turned = jnp.dot(jnp.concatenate(stack, axis=0), to_lane[...], preferred_element_type=jnp.float32)
    for k in range(TERMS + 1):
        at = k // 4 * 384 + k % 4 * 32
        value = turned[at : at + 32] + (turned[at + 128 : at + 160] + turned[at + 256 : at + 288])
        if k < TERMS:
            coefs[k] = value
        else:
            gains[...] = value


def cost(micros):
    return pl.CostEstimate(flops=int(micros * 1e9), bytes_accessed=int(micros * 3.0e6), transcendentals=0)


def body(flux, ivar, pixel_mask, exposure_target, basis, trial_counts, target_class):
    pixels = flux.shape[1]
    tmpl, spec, core = (lax.axis_index(a) for a in AXES)
    place = jnp.stack([core, spec % 2, tmpl // 4, tmpl % 4, spec // 2]).astype(jnp.int32)
    smem = pl.BlockSpec(memory_space=pltpu.SMEM)
    vmem = pl.BlockSpec(memory_space=pltpu.VMEM)
    params = pltpu.CompilerParams(vmem_limit_bytes=VMEM)

    trial = pl.pallas_call(
        prep_kernel,
        out_shape=jax.ShapeDtypeStruct((1, TERMS, SLICES, WIDTH), jnp.bfloat16),
        in_specs=[smem, vmem],
        out_specs=vmem,
        scratch_shapes=[pltpu.VMEM((TERMS * SLICES, WIDTH), jnp.float32)],
        compiler_params=params,
        cost_estimate=cost(0.7),
        name="prep",
    )(place, jnp.transpose(basis, (1, 0, 2)))
    other = send(trial, x_hi=1)
    pair = jnp.concatenate([trial, other], axis=0)

    count = flux.shape[0]
    owners = exposure_target.reshape(1, count)
    views = (flux, ivar, pixel_mask.T, owners)
    keep, outgoing = pl.pallas_call(
        weight_kernel,
        out_shape=(
            jax.ShapeDtypeStruct((count, pixels), jnp.bfloat16),
            jax.ShapeDtypeStruct((count + 16, pixels), jnp.bfloat16),
        ),
        in_specs=[smem] + [pl.BlockSpec(memory_space=pltpu.HBM)] * 4,
        out_specs=(vmem,) * 2,
        scratch_shapes=[pltpu.VMEM(v.shape, v.dtype) for v in views] + [pltpu.SemaphoreType.DMA((8,))],
        compiler_params=params,
        cost_estimate=cost(2.3),
        name="weight",
    )(place, *(pltpu.with_memory_space_constraint(v, pltpu.HBM) for v in views))
    outgoing, _ = lax.optimization_barrier((outgoing, other))
    incoming = send(outgoing, core=1)

    mine = pl.pallas_call(
        coadd_kernel,
        out_shape=jax.ShapeDtypeStruct((64, pixels), jnp.bfloat16),
        in_specs=[smem] + [vmem] * 3,
        out_specs=vmem,
        compiler_params=params,
        cost_estimate=cost(2.4),
        name="coadd",
    )(place, owners, keep, incoming)
    direct = send(mine[:32], x=1), send(mine[32:], x=-1)
    late, _ = lax.optimization_barrier((mine, direct))
    over = send(late, core=1)
    swapped = [send(v, core=1) for v in direct]

    near = [pair] + [send(pair, along=0, step=s) for s in (1, -1, 2)]

    near[0], mine = lax.optimization_barrier((near[0], mine))
    cut = pixels // 256
    eight = pl.pallas_call(
        join_kernel,
        out_shape=tuple(jax.ShapeDtypeStruct((n, HALVES, 16, 128), jnp.bfloat16) for n in (cut, pixels // 128 - cut)),
        in_specs=[vmem] * 4,
        out_specs=(vmem,) * 2,
        compiler_params=params,
        cost_estimate=cost(0.5),
        name="join",
    )(*near)
    up_a, down_b = send(eight[0], along=1, step=1), send(eight[1], along=1, step=-1)
    up_b, down_a = send(eight[1], along=1, step=1), send(eight[0], along=1, step=-1)
    far = send(up_a, along=1, step=1), send(down_b, along=1, step=-1)

    def fit(kernel, operands, shapes, count, micros, name):
        return pl.pallas_call(
            kernel,
            out_shape=shapes,
            in_specs=[smem if v is place else vmem for v in operands],
            out_specs=(vmem,) * len(shapes),
            scratch_shapes=[pltpu.VMEM((count, ROWS, 128), jnp.float32)],
            compiler_params=params,
            cost_estimate=cost(micros),
            name=name,
        )(*operands)

    stack = jax.ShapeDtypeStruct((pixels, 128), jnp.bfloat16)

    def packed(*sizes):
        return jax.ShapeDtypeStruct(sizes + (3, 8, 128), jnp.float32)

    own, *stacks = fit(
        own_fit_kernel, (place, *eight, mine, *direct, over, *swapped), (packed(4, 1), stack, stack), 1, 0, "own_fit"
    )
    (near,) = fit(near_fit_kernel, (up_a, up_b, down_a, down_b, *stacks), (packed(4, 2),), 2, 6, "near_fit")
    parts = fit(far_fit_kernel, (own, near, *far, *stacks), (packed(4),) * 4, 1, 3, "far_fit")

    to_lane, drop = pl.pallas_call(
        trial_order,
        out_shape=(jax.ShapeDtypeStruct((128, 128), jnp.bfloat16), jax.ShapeDtypeStruct((128, 128), jnp.float32)),
        in_specs=[smem, smem, vmem],
        out_specs=(vmem,) * 2,
        compiler_params=params,
        cost_estimate=cost(0),
        name="order",
    )(place, trial_counts, jnp.tile(target_class, 4).reshape(1, 128))
    parts = (
        parts[0],
        send(parts[1], core=1),
        send(parts[2], x=-1),
        send(parts[3], x=1, core=1),
    )
    coefs, gains, best = pl.pallas_call(
        final_kernel,
        out_shape=(
            jax.ShapeDtypeStruct((TERMS, 32, 128), jnp.float32),
            jax.ShapeDtypeStruct((32, 128), jnp.float32),
            jax.ShapeDtypeStruct((1, 32), jnp.float32),
        ),
        in_specs=[vmem] * 6,
        out_specs=(vmem,) * 3,
        compiler_params=params,
        cost_estimate=cost(2),
        name="final",
    )(to_lane, drop, *parts)
    return coefs, gains, best.reshape(32)


def solution(mesh):
    rows = P(AXES, None)
    return jax.shard_map(
        body,
        mesh=mesh,
        in_specs=(rows, rows, rows, P(AXES), P(("tmpl", "spec"), None, None), P(), P(AXES)),
        out_specs=(P(None, AXES, None), P(AXES, None), P(AXES)),
        check_vma=False,
    )
```

```python
import jax
import jax.numpy as jnp
import numpy as np
from jax import lax
from jax.experimental import pallas as pl
from jax.experimental.pallas import tpu as pltpu
from jax.sharding import PartitionSpec as P

AXES = ("tmpl", "spec", "expo")
SIDES = (2, 4, 4, 2, 2)
TERMS = 10
HALVES = TERMS // 2
SLICES = 16
WIDTH = 512
COMBOS = 30
ROWS = COMBOS * 16 + TERMS * 8
VMEM = 24 * 1024 * 1024


def moved(device, core=0, x_hi=0, x=0, along=None, step=0):
    h, z, y, lo, c = (int(v) for v in np.unravel_index(device, SIDES))
    if along is not None:
        if (c == 0) == (along == 0):
            z = (z + step) % 4
        else:
            y = (y + step) % 4
    h, lo = divmod((2 * h + lo + (x if c == 0 else -x)) % 4, 2)
    return int(np.ravel_multi_index((h ^ x_hi, z, y, lo, c ^ core), SIDES))


def send(value, **how):
    return lax.ppermute(value, AXES, [(d, moved(d, **how)) for d in range(128)])


def combos():
    out = [(m, n, 0) for m in range(HALVES) for n in range(m + 1, HALVES)]
    out += [(m, n, 1) for m in range(HALVES) for n in range(m + 1, HALVES)]
    out += [(m, m, 0) for m in range(HALVES)]
    out += [(m, m, 1) for m in range(HALVES)]
    return out


def entry_rows():
    where = {}
    for i, (m, n, crossed) in enumerate(combos()):
        for half in range(2):
            k, l = 2 * m + half, 2 * n + (half ^ crossed)
            where.setdefault((min(k, l), max(k, l)), i * 16 + half * 8)
    return where


def prep_kernel(place, basis, out, rows):
    core = place[0]
    pixels = basis.shape[2]
    tail = pixels - (SLICES - 1) * WIDTH
    rows[...] = jnp.zeros_like(rows)
    for k in range(TERMS):
        both = basis[k].astype(jnp.float32)
        mine = jnp.where(core == 0, both[0:1], both[1:2])
        for h in range(SLICES):
            width = WIDTH if h < SLICES - 1 else tail
            rows[k * SLICES + h : k * SLICES + h + 1, :width] = mine[:, h * WIDTH : h * WIDTH + width]
    out[...] = rows[...].astype(jnp.bfloat16).reshape(out.shape)


def weight_kernel(place, flux, ivar, mask, owner, keep, out, flux_in, ivar_in, mask_in, owner_in, sems):
    core = place[0]
    count, pixels = flux_in.shape
    height = 32
    copies = [(mask, mask_in), (owner, owner_in)]
    for at in range(0, count, height):
        copies += [(a.at[pl.ds(at, height), :], b.at[pl.ds(at, height), :]) for a, b in ((ivar, ivar_in), (flux, flux_in))]
    copies = [pltpu.make_async_copy(a, b, sems.at[i]) for i, (a, b) in enumerate(copies)]
    for copy in copies:
        copy.start()
    copies[0].wait()
    copies[1].wait()
    good = mask_in[...].astype(jnp.float32).T
    names = owner_in[...].astype(jnp.float32)
    out[count : count + 16, :] = jnp.zeros((16, pixels), jnp.bfloat16)
    out[count : count + 16, 0:count] = jnp.broadcast_to(names, (16, count)).astype(jnp.bfloat16)
    for i, at in enumerate(range(0, count, height)):
        copies[2 + 2 * i].wait()
        copies[3 + 2 * i].wait()
        for b in range(good.shape[1]):
            here = slice(at, at + height), slice(b * 128, (b + 1) * 128)
            flag = jnp.broadcast_to(good[at : at + height, b : b + 1], (height, 128)).astype(jnp.bfloat16)
            masked = (ivar_in[here] * flag).astype(jnp.float32)
            fluxes = masked * flux_in[here].astype(jnp.float32)
            keep[here] = jnp.where(core == 0, masked, fluxes).astype(jnp.bfloat16)
            out[here] = jnp.where(core == 0, fluxes, masked).astype(jnp.bfloat16)


def coadd_kernel(place, names, own, other, coadd):
    core = place[0]
    count, pixels = own.shape
    row = lax.broadcasted_iota(jnp.int32, (64, count), 0)
    wanted = jnp.where(row < 32, row + core * 32, row - core * 32).astype(jnp.float32)
    near = (names[...].astype(jnp.float32) == wanted).astype(jnp.float32)
    far = (other[count : count + 16, 0:count][0:1].astype(jnp.float32) == wanted).astype(jnp.float32)
    select = jnp.concatenate([near, far], axis=1).astype(jnp.bfloat16)
    for at in range(0, pixels, WIDTH):
        lanes = slice(at, min(at + WIDTH, pixels))
        spectra = jnp.concatenate([own[:, lanes], other[0:count, lanes]], axis=0)
        coadd[:, lanes] = jnp.dot(select, spectra, preferred_element_type=jnp.float32).astype(jnp.bfloat16)


def join_kernel(own, up, down, far, *halves):
    side = SLICES * 16
    row = lax.broadcasted_iota(jnp.int32, (side, side), 0)
    col = lax.broadcasted_iota(jnp.int32, (side, side), 1)
    same = ((row // 16) == (col % 16)) & ((row % 8) == (col // 32)) & ((row // 8) % 2 == (col // 16) % 2)
    order = same.astype(jnp.float32).astype(jnp.bfloat16)
    for m in range(HALVES):
        block = jnp.concatenate(
            [p[:, 2 * m : 2 * m + 2].reshape(p.shape[0] * 2 * SLICES, WIDTH) for p in (own, up, down, far)], axis=0
        )
        turned = jnp.dot(order, block, preferred_element_type=jnp.float32).astype(jnp.bfloat16)
        cut = halves[0].shape[0]
        for block in range(cut + halves[1].shape[0]):
            h, at = block // 4, block % 4 * 128
            out, place = (halves[0], block) if block < cut else (halves[1], block - cut)
            out[place, m] = turned[h * 16 : h * 16 + 16, at : at + 128]


def solve(entries, right):
    lower, scaled, inverse = {}, {}, []
    for j in range(TERMS):
        pivot = entries[j, j]
        for e in range(j):
            pivot = pivot - lower[j, e] * scaled[j, e]
        inverse.append(1.0 / pivot)
        for i in range(j + 1, TERMS):
            value = entries[j, i]
            for e in range(j):
                value = value - lower[i, e] * scaled[j, e]
            scaled[i, j] = value
            lower[i, j] = value * inverse[j]
    forward = []
    for i in range(TERMS):
        value = right[i]
        for e in range(i):
            value = value - lower[i, e] * forward[e]
        forward.append(value)
    answer = [None] * TERMS
    for i in reversed(range(TERMS)):
        value = forward[i] * inverse[i]
        for e in range(i + 1, TERMS):
            value = value - lower[e, i] * answer[e]
        answer[i] = value
    return answer


def add_up(blocks, begin, count, stacks, total, fresh):
    for at in range(0, count, WIDTH // 128):
        taken = range(at, min(at + WIDTH // 128, count))
        ivar, wflux = stacks(slice((begin + at) * 128, (begin + at + len(taken)) * 128))
        for b, refs in enumerate(blocks):
            evens = []
            for m in range(HALVES):
                pieces = [refs[0][t, m] if t < refs[0].shape[0] else refs[1][t - refs[0].shape[0], m] for t in taken]
                evens.append(jnp.concatenate(pieces, axis=1))
            odds = [jnp.concatenate([e[8:16], e[0:8]], axis=0) for e in evens]
            products = jnp.concatenate(
                [evens[m] * (odds[n] if cross else evens[n]) for m, n, cross in combos()], axis=0
            )
            normal = jnp.dot(products, ivar, preferred_element_type=jnp.float32)
            project = jnp.dot(jnp.concatenate(evens, axis=0), wflux, preferred_element_type=jnp.float32)
            if fresh and at == 0:
                total[b, 0 : COMBOS * 16] = normal
                total[b, COMBOS * 16 : ROWS] = project
            else:
                total[b, 0 : COMBOS * 16] += normal
                total[b, COMBOS * 16 : ROWS] += project


def solve_all(total):
    entries = {}
    for (k, l), at in entry_rows().items():
        value = total[:, at : at + 8, :]
        entries[k, l] = value + 1.0 if k == l else value
    right = [total[:, COMBOS * 16 + k * 8 : COMBOS * 16 + k * 8 + 8, :] for k in range(TERMS)]
    answer = solve(entries, right)
    gain = right[0] * answer[0]
    for k in range(1, TERMS):
        gain = gain + right[k] * answer[k]
    values = answer + [gain / TERMS, jnp.zeros_like(gain)]
    lane = lax.broadcasted_iota(jnp.int32, values[0].shape, 2) // 32
    packed = []
    for group in range(4):
        packed.append([])
        for q in range(3):
            out = None
            for k in range(4):
                shift = (k - group) % 4 * 32
                value = values[4 * q + k]
                value = pltpu.roll(value, shift, 2) if shift else value
                out = value if out is None else jnp.where(lane == k, value, out)
            packed[-1].append(out)
    return packed


def own_fit_kernel(place, own_a, own_b, mine, direct_a, direct_b, over, swapped_a, swapped_b, out, ivar, wflux, total):
    core = place[0]

    def stacks(span):
        near = jnp.concatenate([mine[:, span], direct_a[:, span], direct_b[:, span]], axis=0)
        far = jnp.concatenate([over[32:64, span], over[0:32, span], swapped_b[:, span], swapped_a[:, span]], axis=0)
        both = jnp.where(core == 0, near, far).T, jnp.where(core == 0, far, near).T
        ivar[span, :], wflux[span, :] = both
        return both

    add_up([[own_a, own_b]], 0, mine.shape[1] // 128, stacks, total, True)
    packed = solve_all(total)
    for group in range(4):
        for q in range(3):
            out[group, :, q] = packed[group][q]


def near_fit_kernel(up_a, up_b, down_a, down_b, ivar, wflux, out, total):
    whole = ivar.shape[0] // 128
    add_up([[up_a, up_b], [down_a, down_b]], 0, whole, lambda span: (ivar[span, :], wflux[span, :]), total, True)
    packed = solve_all(total)
    for group in range(4):
        for q in range(3):
            out[group, :, q] = packed[group][q]


def half_fit_kernel(_, far_b, ivar, wflux, total):
    count = far_b.shape[0]
    add_up([[far_b]], ivar.shape[0] // 128 - count, count, lambda span: (ivar[span, :], wflux[span, :]), total, True)


def far_fit_kernel(own, near, half, far_a, ivar, wflux, *rest):
    outs, total = rest[:4], rest[4]
    total[...] = half[...]
    add_up([[far_a]], 0, far_a.shape[0], lambda span: (ivar[span, :], wflux[span, :]), total, False)
    packed = solve_all(total)
    for group in range(4):
        outs[group][0:1] = own[group]
        outs[group][1:3] = near[group]
        for q in range(3):
            outs[group][3:4, q] = packed[group][q]


def trial_order(place, counts, classes, to_lane, drop):
    core, lo, hi, z, y = (place[i] for i in range(5))

    def shift(n):
        return jnp.where(n == 1, 3, jnp.where(n == 2, 1, jnp.where(n == 3, 2, 0)))

    def trial_of(i):
        group, b, t = i // 32, (i // 8) % 4, i % 8
        source_core = core ^ (group % 2)
        source_x = (2 * hi + lo + jnp.where(group < 2, 0, jnp.where(core == 0, 1, 3))) % 4
        near, far = shift(t // 2), shift(b)
        z_of = (z + jnp.where(source_core == 0, near, far)) % 4
        y_of = (y + jnp.where(source_core == 0, far, near)) % 4
        return (source_x // 2 ^ (t % 2)) * 64 + z_of * 16 + y_of * 4 + source_x % 2 * 2 + source_core

    trial = trial_of(lax.broadcasted_iota(jnp.int32, (128, 128), 0))
    lane = lax.broadcasted_iota(jnp.int32, (128, 128), 1)
    to_lane[...] = (trial == lane).astype(jnp.float32).astype(jnp.bfloat16)
    end_0 = counts[0]
    end_1 = end_0 + counts[1]
    end_2 = end_1 + counts[2]
    trial_class = sum((trial >= end).astype(jnp.int32) for end in (end_0, end_1, end_2))
    drop[...] = ((lane // 32 == 2) & (trial_class != classes[...])).astype(jnp.float32)


def final_kernel(to_lane, drop, part_0, part_1, part_2, part_3, coefs, gains, best):
    stack = []
    for q in range(3):
        rows = jnp.concatenate([p[:, q].reshape(32, 128) for p in (part_0, part_1, part_2, part_3)], axis=0)
        if q == 2:
            rows = jnp.where(drop[...] > 0.0, 0.0, rows)
            best[...] = jnp.max(rows, axis=0, keepdims=True)[:, 64:96]
        rest = rows.T
        for _ in range(3):
            part = rest.astype(jnp.bfloat16)
            stack.append(part)
            rest = rest - part.astype(jnp.float32)
    turned = jnp.dot(jnp.concatenate(stack, axis=0), to_lane[...], preferred_element_type=jnp.float32)
    for k in range(TERMS + 1):
        at = k // 4 * 384 + k % 4 * 32
        value = turned[at : at + 32] + (turned[at + 128 : at + 160] + turned[at + 256 : at + 288])
        if k < TERMS:
            coefs[k] = value
        else:
            gains[...] = value


def cost(micros):
    return pl.CostEstimate(flops=int(micros * 1e9), bytes_accessed=int(micros * 3.0e6), transcendentals=0)


def body(flux, ivar, pixel_mask, exposure_target, basis, trial_counts, target_class):
    pixels = flux.shape[1]
    tmpl, spec, core = (lax.axis_index(a) for a in AXES)
    place = jnp.stack([core, spec % 2, tmpl // 4, tmpl % 4, spec // 2]).astype(jnp.int32)
    smem = pl.BlockSpec(memory_space=pltpu.SMEM)
    vmem = pl.BlockSpec(memory_space=pltpu.VMEM)
    params = pltpu.CompilerParams(vmem_limit_bytes=VMEM)

    trial = pl.pallas_call(
        prep_kernel,
        out_shape=jax.ShapeDtypeStruct((1, TERMS, SLICES, WIDTH), jnp.bfloat16),
        in_specs=[smem, vmem],
        out_specs=vmem,
        scratch_shapes=[pltpu.VMEM((TERMS * SLICES, WIDTH), jnp.float32)],
        compiler_params=params,
        cost_estimate=cost(0.7),
        name="prep",
    )(place, jnp.transpose(basis, (1, 0, 2)))
    other = send(trial, x_hi=1)
    pair = jnp.concatenate([trial, other], axis=0)

    count = flux.shape[0]
    owners = exposure_target.reshape(1, count)
    views = (flux, ivar, pixel_mask.T, owners)
    keep, outgoing = pl.pallas_call(
        weight_kernel,
        out_shape=(
            jax.ShapeDtypeStruct((count, pixels), jnp.bfloat16),
            jax.ShapeDtypeStruct((count + 16, pixels), jnp.bfloat16),
        ),
        in_specs=[smem] + [pl.BlockSpec(memory_space=pltpu.HBM)] * 4,
        out_specs=(vmem,) * 2,
        scratch_shapes=[pltpu.VMEM(v.shape, v.dtype) for v in views] + [pltpu.SemaphoreType.DMA((8,))],
        compiler_params=params,
        cost_estimate=cost(2.3),
        name="weight",
    )(place, *(pltpu.with_memory_space_constraint(v, pltpu.HBM) for v in views))
    outgoing, _ = lax.optimization_barrier((outgoing, other))
    incoming = send(outgoing, core=1)

    mine = pl.pallas_call(
        coadd_kernel,
        out_shape=jax.ShapeDtypeStruct((64, pixels), jnp.bfloat16),
        in_specs=[smem] + [vmem] * 3,
        out_specs=vmem,
        compiler_params=params,
        cost_estimate=cost(2.4),
        name="coadd",
    )(place, owners, keep, incoming)
    direct = send(mine[:32], x=1), send(mine[32:], x=-1)
    late, _ = lax.optimization_barrier((mine, direct))
    over = send(late, core=1)
    swapped = [send(v, core=1) for v in direct]

    near = [pair] + [send(pair, along=0, step=s) for s in (1, -1, 2)]

    near[0], mine = lax.optimization_barrier((near[0], mine))
    cut = pixels // 256
    eight = pl.pallas_call(
        join_kernel,
        out_shape=tuple(jax.ShapeDtypeStruct((n, HALVES, 16, 128), jnp.bfloat16) for n in (cut, pixels // 128 - cut)),
        in_specs=[vmem] * 4,
        out_specs=(vmem,) * 2,
        compiler_params=params,
        cost_estimate=cost(0.5),
        name="join",
    )(*near)
    up_a, down_b = send(eight[0], along=1, step=1), send(eight[1], along=1, step=-1)
    up_b, down_a = send(eight[1], along=1, step=1), send(eight[0], along=1, step=-1)
    far = send(up_a, along=1, step=1), send(down_b, along=1, step=-1)

    def fit(kernel, operands, shapes, count, micros, name):
        return pl.pallas_call(
            kernel,
            out_shape=shapes,
            in_specs=[smem if v is place else vmem for v in operands],
            out_specs=(vmem,) * len(shapes),
            scratch_shapes=[pltpu.VMEM((count, ROWS, 128), jnp.float32)],
            compiler_params=params,
            cost_estimate=cost(micros),
            name=name,
        )(*operands)

    stack = jax.ShapeDtypeStruct((pixels, 128), jnp.bfloat16)

    def packed(*sizes):
        return jax.ShapeDtypeStruct(sizes + (3, 8, 128), jnp.float32)

    own, *stacks = fit(
        own_fit_kernel, (place, *eight, mine, *direct, over, *swapped), (packed(4, 1), stack, stack), 1, 0, "own_fit"
    )
    (near,) = fit(near_fit_kernel, (up_a, up_b, down_a, down_b, *stacks), (packed(4, 2),), 2, 6, "near_fit")
    half = pl.pallas_call(
        half_fit_kernel,
        out_shape=jax.ShapeDtypeStruct((1, ROWS, 128), jnp.float32),
        in_specs=[pl.BlockSpec(memory_space=pl.ANY)] + [vmem] * 3,
        out_specs=vmem,
        compiler_params=params,
        cost_estimate=cost(0),
        name="half_fit",
    )(near, far[1], *stacks)
    parts = fit(far_fit_kernel, (own, near, half, far[0], *stacks), (packed(4),) * 4, 1, 3, "far_fit")

    to_lane, drop = pl.pallas_call(
        trial_order,
        out_shape=(jax.ShapeDtypeStruct((128, 128), jnp.bfloat16), jax.ShapeDtypeStruct((128, 128), jnp.float32)),
        in_specs=[smem, smem, vmem],
        out_specs=(vmem,) * 2,
        compiler_params=params,
        cost_estimate=cost(0),
        name="order",
    )(place, trial_counts, jnp.tile(target_class, 4).reshape(1, 128))
    parts = (
        parts[0],
        send(parts[1], core=1),
        send(parts[2], x=-1),
        send(parts[3], x=1, core=1),
    )
    coefs, gains, best = pl.pallas_call(
        final_kernel,
        out_shape=(
            jax.ShapeDtypeStruct((TERMS, 32, 128), jnp.float32),
            jax.ShapeDtypeStruct((32, 128), jnp.float32),
            jax.ShapeDtypeStruct((1, 32), jnp.float32),
        ),
        in_specs=[vmem] * 6,
        out_specs=(vmem,) * 3,
        compiler_params=params,
        cost_estimate=cost(2),
        name="final",
    )(to_lane, drop, *parts)
    return coefs, gains, best.reshape(32)


def solution(mesh):
    rows = P(AXES, None)
    return jax.shard_map(
        body,
        mesh=mesh,
        in_specs=(rows, rows, rows, P(AXES), P(("tmpl", "spec"), None, None), P(), P(AXES)),
        out_specs=(P(None, AXES, None), P(AXES, None), P(AXES)),
        check_vma=False,
    )
```

```python
import jax
import jax.numpy as jnp
import numpy as np
from jax import lax
from jax.experimental import pallas as pl
from jax.experimental.pallas import tpu as pltpu
from jax.sharding import PartitionSpec as P

AXES = ("tmpl", "spec", "expo")
SIDES = (2, 4, 4, 2, 2)
TERMS = 10
HALVES = TERMS // 2
SLICES = 16
WIDTH = 512
COMBOS = 30
ROWS = COMBOS * 16 + TERMS * 8
VMEM = 24 * 1024 * 1024


def moved(device, core=0, x_hi=0, x=0, along=None, step=0):
    h, z, y, lo, c = (int(v) for v in np.unravel_index(device, SIDES))
    if along is not None:
        if (c == 0) == (along == 0):
            z = (z + step) % 4
        else:
            y = (y + step) % 4
    h, lo = divmod((2 * h + lo + (x if c == 0 else -x)) % 4, 2)
    return int(np.ravel_multi_index((h ^ x_hi, z, y, lo, c ^ core), SIDES))


def send(value, **how):
    return lax.ppermute(value, AXES, [(d, moved(d, **how)) for d in range(128)])


def combos():
    out = [(m, n, 0) for m in range(HALVES) for n in range(m + 1, HALVES)]
    out += [(m, n, 1) for m in range(HALVES) for n in range(m + 1, HALVES)]
    out += [(m, m, 0) for m in range(HALVES)]
    out += [(m, m, 1) for m in range(HALVES)]
    return out


def entry_rows():
    where = {}
    for i, (m, n, crossed) in enumerate(combos()):
        for half in range(2):
            k, l = 2 * m + half, 2 * n + (half ^ crossed)
            where.setdefault((min(k, l), max(k, l)), i * 16 + half * 8)
    return where


def prep_kernel(place, basis, out, rows):
    core = place[0]
    pixels = basis.shape[2]
    tail = pixels - (SLICES - 1) * WIDTH
    rows[...] = jnp.zeros_like(rows)
    for k in range(TERMS):
        both = basis[k].astype(jnp.float32)
        mine = jnp.where(core == 0, both[0:1], both[1:2])
        for h in range(SLICES):
            width = WIDTH if h < SLICES - 1 else tail
            rows[k * SLICES + h : k * SLICES + h + 1, :width] = mine[:, h * WIDTH : h * WIDTH + width]
    out[...] = rows[...].astype(jnp.bfloat16).reshape(out.shape)


def weight_kernel(place, flux, ivar, mask, owner, keep, out, flux_in, ivar_in, mask_in, owner_in, sems):
    core = place[0]
    count, pixels = flux_in.shape
    height = 32
    copies = [(mask, mask_in), (owner, owner_in)]
    for at in range(0, count, height):
        copies += [(a.at[pl.ds(at, height), :], b.at[pl.ds(at, height), :]) for a, b in ((ivar, ivar_in), (flux, flux_in))]
    copies = [pltpu.make_async_copy(a, b, sems.at[i]) for i, (a, b) in enumerate(copies)]
    for copy in copies:
        copy.start()
    copies[0].wait()
    copies[1].wait()
    good = mask_in[...].astype(jnp.float32).T
    names = owner_in[...].astype(jnp.float32)
    out[count : count + 16, :] = jnp.zeros((16, pixels), jnp.bfloat16)
    out[count : count + 16, 0:count] = jnp.broadcast_to(names, (16, count)).astype(jnp.bfloat16)
    for i, at in enumerate(range(0, count, height)):
        copies[2 + 2 * i].wait()
        copies[3 + 2 * i].wait()
        for b in range(good.shape[1]):
            here = slice(at, at + height), slice(b * 128, (b + 1) * 128)
            flag = jnp.broadcast_to(good[at : at + height, b : b + 1], (height, 128)).astype(jnp.bfloat16)
            masked = (ivar_in[here] * flag).astype(jnp.float32)
            fluxes = masked * flux_in[here].astype(jnp.float32)
            keep[here] = jnp.where(core == 0, masked, fluxes).astype(jnp.bfloat16)
            out[here] = jnp.where(core == 0, fluxes, masked).astype(jnp.bfloat16)


def coadd_kernel(place, names, own, other, coadd):
    core = place[0]
    count, pixels = own.shape
    row = lax.broadcasted_iota(jnp.int32, (64, count), 0)
    wanted = jnp.where(row < 32, row + core * 32, row - core * 32).astype(jnp.float32)
    near = (names[...].astype(jnp.float32) == wanted).astype(jnp.float32)
    far = (other[count : count + 16, 0:count][0:1].astype(jnp.float32) == wanted).astype(jnp.float32)
    select = jnp.concatenate([near, far], axis=1).astype(jnp.bfloat16)
    for at in range(0, pixels, WIDTH):
        lanes = slice(at, min(at + WIDTH, pixels))
        spectra = jnp.concatenate([own[:, lanes], other[0:count, lanes]], axis=0)
        coadd[:, lanes] = jnp.dot(select, spectra, preferred_element_type=jnp.float32).astype(jnp.bfloat16)


def join_kernel(own, far, up, down, *halves):
    side = SLICES * 16
    row = lax.broadcasted_iota(jnp.int32, (side, side), 0)
    col = lax.broadcasted_iota(jnp.int32, (side, side), 1)
    same = ((row // 16) == (col % 16)) & ((row % 8) == (col // 32)) & ((row // 8) % 2 == (col // 16) % 2)
    order = same.astype(jnp.float32).astype(jnp.bfloat16)
    for m in range(HALVES):
        block = jnp.concatenate(
            [p[:, 2 * m : 2 * m + 2].reshape(p.shape[0] * 2 * SLICES, WIDTH) for p in (own, up, down, far)], axis=0
        )
        turned = jnp.dot(order, block, preferred_element_type=jnp.float32).astype(jnp.bfloat16)
        cut = halves[0].shape[0]
        for block in range(cut + halves[1].shape[0]):
            h, at = block // 4, block % 4 * 128
            out, place = (halves[0], block) if block < cut else (halves[1], block - cut)
            out[place, m] = turned[h * 16 : h * 16 + 16, at : at + 128]


def solve(entries, right):
    lower, scaled, inverse = {}, {}, []
    for j in range(TERMS):
        pivot = entries[j, j]
        for e in range(j):
            pivot = pivot - lower[j, e] * scaled[j, e]
        inverse.append(1.0 / pivot)
        for i in range(j + 1, TERMS):
            value = entries[j, i]
            for e in range(j):
                value = value - lower[i, e] * scaled[j, e]
            scaled[i, j] = value
            lower[i, j] = value * inverse[j]
    forward = []
    for i in range(TERMS):
        value = right[i]
        for e in range(i):
            value = value - lower[i, e] * forward[e]
        forward.append(value)
    answer = [None] * TERMS
    for i in reversed(range(TERMS)):
        value = forward[i] * inverse[i]
        for e in range(i + 1, TERMS):
            value = value - lower[e, i] * answer[e]
        answer[i] = value
    return answer


def add_up(blocks, begin, count, stacks, total, fresh):
    for at in range(0, count, WIDTH // 128):
        taken = range(at, min(at + WIDTH // 128, count))
        ivar, wflux = stacks(slice((begin + at) * 128, (begin + at + len(taken)) * 128))
        for b, refs in enumerate(blocks):
            evens = []
            for m in range(HALVES):
                pieces = [refs[0][t, m] if t < refs[0].shape[0] else refs[1][t - refs[0].shape[0], m] for t in taken]
                evens.append(jnp.concatenate(pieces, axis=1))
            odds = [jnp.concatenate([e[8:16], e[0:8]], axis=0) for e in evens]
            products = jnp.concatenate(
                [evens[m] * (odds[n] if cross else evens[n]) for m, n, cross in combos()], axis=0
            )
            normal = jnp.dot(products, ivar, preferred_element_type=jnp.float32)
            project = jnp.dot(jnp.concatenate(evens, axis=0), wflux, preferred_element_type=jnp.float32)
            if fresh and at == 0:
                total[b, 0 : COMBOS * 16] = normal
                total[b, COMBOS * 16 : ROWS] = project
            else:
                total[b, 0 : COMBOS * 16] += normal
                total[b, COMBOS * 16 : ROWS] += project


def solve_all(total):
    entries = {}
    for (k, l), at in entry_rows().items():
        value = total[:, at : at + 8, :]
        entries[k, l] = value + 1.0 if k == l else value
    right = [total[:, COMBOS * 16 + k * 8 : COMBOS * 16 + k * 8 + 8, :] for k in range(TERMS)]
    answer = solve(entries, right)
    gain = right[0] * answer[0]
    for k in range(1, TERMS):
        gain = gain + right[k] * answer[k]
    values = answer + [gain / TERMS, jnp.zeros_like(gain)]
    lane = lax.broadcasted_iota(jnp.int32, values[0].shape, 2) // 32
    packed = []
    for group in range(4):
        packed.append([])
        for q in range(3):
            out = None
            for k in range(4):
                shift = (k - group) % 4 * 32
                value = values[4 * q + k]
                value = pltpu.roll(value, shift, 2) if shift else value
                out = value if out is None else jnp.where(lane == k, value, out)
            packed[-1].append(out)
    return packed


def own_fit_kernel(place, own_a, own_b, mine, direct_a, direct_b, over, swapped_a, swapped_b, out, ivar, wflux, total):
    core = place[0]

    def stacks(span):
        near = jnp.concatenate([mine[:, span], direct_a[:, span], direct_b[:, span]], axis=0)
        far = jnp.concatenate([over[32:64, span], over[0:32, span], swapped_b[:, span], swapped_a[:, span]], axis=0)
        both = jnp.where(core == 0, near, far).T, jnp.where(core == 0, far, near).T
        ivar[span, :], wflux[span, :] = both
        return both

    add_up([[own_a, own_b]], 0, mine.shape[1] // 128, stacks, total, True)
    packed = solve_all(total)
    for group in range(4):
        for q in range(3):
            out[group, :, q] = packed[group][q]


def near_fit_kernel(up_a, up_b, down_a, down_b, ivar, wflux, out, total):
    whole = ivar.shape[0] // 128
    add_up([[up_a, up_b], [down_a, down_b]], 0, whole, lambda span: (ivar[span, :], wflux[span, :]), total, True)
    packed = solve_all(total)
    for group in range(4):
        for q in range(3):
            out[group, :, q] = packed[group][q]


def half_fit_kernel(_, far_b, ivar, wflux, total):
    count = far_b.shape[0]
    add_up([[far_b]], ivar.shape[0] // 128 - count, count, lambda span: (ivar[span, :], wflux[span, :]), total, True)


def far_fit_kernel(own, near, half, far_a, ivar, wflux, *rest):
    outs, total = rest[:4], rest[4]
    total[...] = half[...]
    add_up([[far_a]], 0, far_a.shape[0], lambda span: (ivar[span, :], wflux[span, :]), total, False)
    packed = solve_all(total)
    for group in range(4):
        outs[group][0:1] = own[group]
        outs[group][1:3] = near[group]
        for q in range(3):
            outs[group][3:4, q] = packed[group][q]


def trial_order(place, counts, classes, to_lane, drop):
    core, lo, hi, z, y = (place[i] for i in range(5))

    def shift(n):
        return jnp.where(n == 1, 3, jnp.where(n == 2, 1, jnp.where(n == 3, 2, 0)))

    def trial_of(i):
        group, b, t = i // 32, (i // 8) % 4, i % 8
        source_core = core ^ (group % 2)
        source_x = (2 * hi + lo + jnp.where(group < 2, 0, jnp.where(core == 0, 1, 3))) % 4
        near, far = shift(t // 2), shift(b)
        z_of = (z + jnp.where(source_core == 0, near, far)) % 4
        y_of = (y + jnp.where(source_core == 0, far, near)) % 4
        return (source_x // 2 ^ (t % 2)) * 64 + z_of * 16 + y_of * 4 + source_x % 2 * 2 + source_core

    trial = trial_of(lax.broadcasted_iota(jnp.int32, (128, 128), 0))
    lane = lax.broadcasted_iota(jnp.int32, (128, 128), 1)
    to_lane[...] = (trial == lane).astype(jnp.float32).astype(jnp.bfloat16)
    end_0 = counts[0]
    end_1 = end_0 + counts[1]
    end_2 = end_1 + counts[2]
    trial_class = sum((trial >= end).astype(jnp.int32) for end in (end_0, end_1, end_2))
    drop[...] = ((lane // 32 == 2) & (trial_class != classes[...])).astype(jnp.float32)


def final_kernel(to_lane, drop, part_0, part_1, part_2, part_3, coefs, gains, best):
    stack = []
    for q in range(3):
        rows = jnp.concatenate([p[:, q].reshape(32, 128) for p in (part_0, part_1, part_2, part_3)], axis=0)
        if q == 2:
            rows = jnp.where(drop[...] > 0.0, 0.0, rows)
            best[...] = jnp.max(rows, axis=0, keepdims=True)[:, 64:96]
        rest = rows.T
        for _ in range(3):
            part = rest.astype(jnp.bfloat16)
            stack.append(part)
            rest = rest - part.astype(jnp.float32)
    turned = jnp.dot(jnp.concatenate(stack, axis=0), to_lane[...], preferred_element_type=jnp.float32)
    for k in range(TERMS + 1):
        at = k // 4 * 384 + k % 4 * 32
        value = turned[at : at + 32] + (turned[at + 128 : at + 160] + turned[at + 256 : at + 288])
        if k < TERMS:
            coefs[k] = value
        else:
            gains[...] = value


def cost(micros):
    return pl.CostEstimate(flops=int(micros * 1e9), bytes_accessed=int(micros * 3.0e6), transcendentals=0)


def body(flux, ivar, pixel_mask, exposure_target, basis, trial_counts, target_class):
    pixels = flux.shape[1]
    tmpl, spec, core = (lax.axis_index(a) for a in AXES)
    place = jnp.stack([core, spec % 2, tmpl // 4, tmpl % 4, spec // 2]).astype(jnp.int32)
    smem = pl.BlockSpec(memory_space=pltpu.SMEM)
    vmem = pl.BlockSpec(memory_space=pltpu.VMEM)
    params = pltpu.CompilerParams(vmem_limit_bytes=VMEM)

    trial = pl.pallas_call(
        prep_kernel,
        out_shape=jax.ShapeDtypeStruct((1, TERMS, SLICES, WIDTH), jnp.bfloat16),
        in_specs=[smem, vmem],
        out_specs=vmem,
        scratch_shapes=[pltpu.VMEM((TERMS * SLICES, WIDTH), jnp.float32)],
        compiler_params=params,
        cost_estimate=cost(0.7),
        name="prep",
    )(place, jnp.transpose(basis, (1, 0, 2)))
    other = send(trial, x_hi=1)
    pair = jnp.concatenate([trial, other], axis=0)

    count = flux.shape[0]
    owners = exposure_target.reshape(1, count)
    views = (flux, ivar, pixel_mask.T, owners)
    keep, outgoing = pl.pallas_call(
        weight_kernel,
        out_shape=(
            jax.ShapeDtypeStruct((count, pixels), jnp.bfloat16),
            jax.ShapeDtypeStruct((count + 16, pixels), jnp.bfloat16),
        ),
        in_specs=[smem] + [pl.BlockSpec(memory_space=pltpu.HBM)] * 4,
        out_specs=(vmem,) * 2,
        scratch_shapes=[pltpu.VMEM(v.shape, v.dtype) for v in views] + [pltpu.SemaphoreType.DMA((8,))],
        compiler_params=params,
        cost_estimate=cost(2.3),
        name="weight",
    )(place, *(pltpu.with_memory_space_constraint(v, pltpu.HBM) for v in views))
    outgoing, _ = lax.optimization_barrier((outgoing, other))
    incoming = send(outgoing, core=1)

    mine = pl.pallas_call(
        coadd_kernel,
        out_shape=jax.ShapeDtypeStruct((64, pixels), jnp.bfloat16),
        in_specs=[smem] + [vmem] * 3,
        out_specs=vmem,
        compiler_params=params,
        cost_estimate=cost(2.4),
        name="coadd",
    )(place, owners, keep, incoming)
    direct = send(mine[:32], x=1), send(mine[32:], x=-1)
    late, _ = lax.optimization_barrier((mine, direct))
    over = send(late, core=1)
    swapped = [send(v, core=1) for v in direct]

    near = [send(pair, along=0, step=s) for s in (2, 1, -1)]
    near = [pair] + near

    near[0], mine = lax.optimization_barrier((near[0], mine))
    cut = pixels // 256
    eight = pl.pallas_call(
        join_kernel,
        out_shape=tuple(jax.ShapeDtypeStruct((n, HALVES, 16, 128), jnp.bfloat16) for n in (cut, pixels // 128 - cut)),
        in_specs=[vmem] * 4,
        out_specs=(vmem,) * 2,
        compiler_params=params,
        cost_estimate=cost(0.5),
        name="join",
    )(*near)
    up_a, down_b = send(eight[0], along=1, step=1), send(eight[1], along=1, step=-1)
    up_b, down_a = send(eight[1], along=1, step=1), send(eight[0], along=1, step=-1)
    far = send(up_a, along=1, step=1), send(down_b, along=1, step=-1)

    def fit(kernel, operands, shapes, count, micros, name):
        return pl.pallas_call(
            kernel,
            out_shape=shapes,
            in_specs=[smem if v is place else vmem for v in operands],
            out_specs=(vmem,) * len(shapes),
            scratch_shapes=[pltpu.VMEM((count, ROWS, 128), jnp.float32)],
            compiler_params=params,
            cost_estimate=cost(micros),
            name=name,
        )(*operands)

    stack = jax.ShapeDtypeStruct((pixels, 128), jnp.bfloat16)

    def packed(*sizes):
        return jax.ShapeDtypeStruct(sizes + (3, 8, 128), jnp.float32)

    own, *stacks = fit(
        own_fit_kernel, (place, *eight, mine, *direct, over, *swapped), (packed(4, 1), stack, stack), 1, 0, "own_fit"
    )
    (near,) = fit(near_fit_kernel, (up_a, up_b, down_a, down_b, *stacks), (packed(4, 2),), 2, 6, "near_fit")
    half = pl.pallas_call(
        half_fit_kernel,
        out_shape=jax.ShapeDtypeStruct((1, ROWS, 128), jnp.float32),
        in_specs=[pl.BlockSpec(memory_space=pl.ANY)] + [vmem] * 3,
        out_specs=vmem,
        compiler_params=params,
        cost_estimate=cost(0),
        name="half_fit",
    )(near, far[1], *stacks)
    parts = fit(far_fit_kernel, (own, near, half, far[0], *stacks), (packed(4),) * 4, 1, 3, "far_fit")

    to_lane, drop = pl.pallas_call(
        trial_order,
        out_shape=(jax.ShapeDtypeStruct((128, 128), jnp.bfloat16), jax.ShapeDtypeStruct((128, 128), jnp.float32)),
        in_specs=[smem, smem, vmem],
        out_specs=(vmem,) * 2,
        compiler_params=params,
        cost_estimate=cost(0),
        name="order",
    )(place, trial_counts, jnp.tile(target_class, 4).reshape(1, 128))
    parts = (
        parts[0],
        send(parts[1], core=1),
        send(parts[2], x=-1),
        send(parts[3], x=1, core=1),
    )
    coefs, gains, best = pl.pallas_call(
        final_kernel,
        out_shape=(
            jax.ShapeDtypeStruct((TERMS, 32, 128), jnp.float32),
            jax.ShapeDtypeStruct((32, 128), jnp.float32),
            jax.ShapeDtypeStruct((1, 32), jnp.float32),
        ),
        in_specs=[vmem] * 6,
        out_specs=(vmem,) * 3,
        compiler_params=params,
        cost_estimate=cost(2),
        name="final",
    )(to_lane, drop, *parts)
    return coefs, gains, best.reshape(32)


def solution(mesh):
    rows = P(AXES, None)
    return jax.shard_map(
        body,
        mesh=mesh,
        in_specs=(rows, rows, rows, P(AXES), P(("tmpl", "spec"), None, None), P(), P(AXES)),
        out_specs=(P(None, AXES, None), P(AXES, None), P(AXES)),
        check_vma=False,
    )
```
